32 devices in a mesh: dp: 8 (over z, x), layer: 4 (over y, core).
Axes of the slice: x: 2, y: 2, z: 4, core: 2. Of those that a mesh axis runs over, the one named last changes fastest.
Arguments:
- audio_in: float32 [8, 49152], P(None, 'dp'), may hold values from -6 to 6
- mel_spec: bfloat16 [80, 49152], P(None, 'dp'), may hold values from -6 to 6
- lengths: int32 [32, 4], P('dp'), may hold values from 1 to 1024, 1536 in all within a row
- z_cotangent: float32 [8, 49152], P(None, 'dp'), may hold values from -6 to 6
- det_cotangent: float32 [49152], P('dp'), may hold values from -6 to 6
- lu_weight: float32 [8, 8], replicated, may hold values from -1.2 to 1.2
- start_weight: float32 [512, 4], replicated, may hold values from -3 to 3
- start_bias: float32 [512], replicated, may hold values from -3 to 3
- in_weight: bfloat16 [4, 1024, 1536], P('layer'), may hold values from -0.15625 to 0.15625
- cond_weight: bfloat16 [4, 1024, 80], P('layer'), may hold values from -0.625 to 0.625
- gate_bias: float32 [4, 1024], P('layer'), may hold values from -3 to 3
- mix_weight: bfloat16 [4, 768, 512], P('layer'), may hold values from -0.25 to 0.25
- mix_bias: float32 [4, 768], P('layer'), may hold values from -2 to 2
- end_weight: bfloat16 [8, 768], replicated, may hold values from -0.109375 to 0.109375
- end_bias: float32 [8], replicated, may hold values from -1.5 to 1.5
Outputs:
- latent: float32 [8, 49152], P(None, ('dp', 'layer'))
- logdet: float32 [49152], P(('dp', 'layer'))
- audio_grad: float32 [8, 49152], P(None, ('dp', 'layer'))
- mel_grad: float32 [80, 49152], P(None, ('dp', 'layer'))
- lu_grad: float32 [8, 8], replicated
- start_weight_grad: float32 [512, 4], replicated
- start_bias_grad: float32 [512], replicated
- in_weight_grad: float32 [4, 1024, 1536], P('layer', 'dp')
- cond_weight_grad: float32 [4, 1024, 80], P('layer', 'dp')
- gate_bias_grad: float32 [4, 1024], P('layer', 'dp')
- mix_weight_grad: float32 [4, 768, 512], P('layer', 'dp')
- mix_bias_grad: float32 [4, 768], P('layer', 'dp')
- end_weight_grad: float32 [8, 768], replicated
- end_bias_grad: float32 [8], replicated
The draws below stay inside these ranges and needn't reach their ends.
Inputs may be any that keep to these rules, and one draw needn't show every extreme that they name: `lengths`: each row sums to 1536 exactly and its largest entry is 1024.
All inputs are finite; a program needn't handle non-finite values.
Results may differ from the reference program's by a relative error of at most 0.023.
Values may be sent and summed in bfloat16 or wider, within the bound.
No kernel may reach another device: no remote copies, remote signals or barrier semaphores. Data moves between devices by JAX's collectives and lax.ppermute only.
A program may use at most 320 MiB of HBM per device.

```python
import math
import jax
import jax.numpy as jnp
import numpy as np
from jax import lax

GROUP = 8
HALF = 4
RES = 512
SKIP = 256
GATE = 1024
MEL = 80
KERNEL = 3
LAYERS = 4
MB_ROWS = 1536
UTTS = 4
LONGEST = 1024
BATCHES = 32
FRAMES = 49152


def block_scale(key, dims, split, least, high):
    factor_of, own = 1.0, jax.random.fold_in(key, 6)
    for dim, blocks in split:
        draws = jnp.exp(jax.random.uniform(jax.random.fold_in(own, dim), (blocks,), jnp.float32, least / len(split), high / len(split)))
        factor_of = factor_of * jnp.repeat(draws, dims[dim] // blocks).reshape([-1 if axis == dim else 1 for axis in range(len(dims))])
    return factor_of


def length_profile(number_of, total, most, lean):
    loads = [(1 << 20) // math.isqrt(standing ** lean) + 1 for standing in range(2, number_of + 1)]
    spare, given = total - most - (number_of - 1), [1] * (number_of - 1)
    while spare > 0:
        free = [i for i in range(number_of - 1) if given[i] < most]
        pool, remaining = sum([loads[i] for i in free]), spare
        for i in free:
            more = min(most - given[i], max(1, remaining * loads[i] // pool), spare)
            given[i] = given[i] + more
            spare = spare - more
    return np.array([most] + given)


def ragged(key, count, total, limit, lean):
    if count == 2:
        one = jax.random.randint(key, (), max(1, total - limit), min(limit, total - 1) + 1)
        return jnp.stack([one, total - one])
    sizes = jnp.asarray(length_profile(count, total, limit, lean), jnp.int32)
    pairs = (count - 1) // 2
    source_of, sink = sizes[1:1 + 2 * pairs:2], sizes[2:2 + 2 * pairs:2]
    slack = jnp.minimum(source_of - 1, limit - sink)
    passed = jax.random.randint(jax.random.fold_in(key, 1), (pairs,), 0, 1 << 20) % (slack + 1)
    sizes = sizes.at[1:1 + 2 * pairs:2].set(source_of - passed).at[2:2 + 2 * pairs:2].set(sink + passed)
    return sizes[jax.random.permutation(jax.random.fold_in(key, 2), count)]


def normal_values(key, dims, width, most, split=(), kind=jnp.bfloat16):
    entries = width * jax.random.normal(key, dims, jnp.float32)
    if split:
        entries = entries * block_scale(key, dims, split, -0.22, 0.18)
    return jnp.clip(entries, -most, most).astype(kind)


def setup_inputs(seed: int = 0) -> dict:
    keys = jax.random.split(jax.random.key(seed), 16)
    return {
        "audio_in": normal_values(keys[0], (GROUP, FRAMES), 1.0, 6.0, ((1, 8),), jnp.float32),
        "mel_spec": normal_values(keys[1], (MEL, FRAMES), 1.0, 6.0, ((1, 8),)),
        "lengths": jax.vmap(lambda own: ragged(own, UTTS, MB_ROWS, LONGEST, 2))(jax.random.split(keys[2], BATCHES)).reshape((BATCHES, UTTS)).astype(jnp.int32),
        "z_cotangent": normal_values(keys[3], (GROUP, FRAMES), 1.0, 6.0, ((1, 8),), jnp.float32),
        "det_cotangent": normal_values(keys[4], (FRAMES,), 1.0, 6.0, ((0, 8),), jnp.float32),
        "lu_weight": normal_values(keys[5], (GROUP, GROUP), 0.3, 1.2, (), jnp.float32),
        "start_weight": normal_values(keys[6], (RES, HALF), HALF ** -0.5, 3.0, (), jnp.float32),
        "start_bias": normal_values(keys[7], (RES,), 0.5, 3.0, (), jnp.float32),
        "in_weight": normal_values(keys[8], (LAYERS, GATE, KERNEL * RES), (KERNEL * RES) ** -0.5, 0.15625, ((0, 4),)),
        "cond_weight": normal_values(keys[9], (LAYERS, GATE, MEL), MEL ** -0.5, 0.625, ((0, 4),)),
        "gate_bias": normal_values(keys[10], (LAYERS, GATE), 0.5, 3.0, ((0, 4),), jnp.float32),
        "mix_weight": normal_values(keys[11], (LAYERS, RES + SKIP, RES), RES ** -0.5, 0.25, ((0, 4),)),
        "mix_bias": normal_values(keys[12], (LAYERS, RES + SKIP), 0.3, 2.0, ((0, 4),), jnp.float32),
        "end_weight": normal_values(keys[13], (GROUP, RES + SKIP), (4 * (RES + SKIP)) ** -0.5, 0.109375),
        "end_bias": normal_values(keys[14], (GROUP,), 0.3, 1.5, (), jnp.float32),
    }


highest = lax.Precision.HIGHEST

@jax.custom_vjp
def low(v):
    return lax.optimization_barrier(v.astype(jnp.bfloat16)).astype(jnp.float32)

@jax.custom_vjp
def low_back(v):
    return v

def low_keep(v):
    return (low(v), None)

def low_pass(kept, grad):
    return (grad,)

def back_keep(v):
    return (v, None)

def back_low(kept, grad):
    return (low(grad),)
low.defvjp(low_keep, low_pass)
low_back.defvjp(back_keep, back_low)

def flow_matrix(lu_weight):
    size_now = lu_weight.shape[0]
    lower = jnp.tril(lu_weight, -1) + jnp.eye(size_now, dtype=lu_weight.dtype)
    upper = jnp.triu(lu_weight, 1) + jnp.diag(jnp.exp(jnp.diagonal(lu_weight)))
    return jnp.dot(lower, upper, precision=highest)

def rooms(length_row, row_count):
    ends = jnp.cumsum(length_row).astype(jnp.int32)
    starts = (ends - length_row).astype(jnp.int32)
    places = jnp.arange(row_count, dtype=jnp.int32)[None, :]
    inside = (places >= starts[:, None]) & (places < ends[:, None])
    left_room = lax.optimization_barrier(jnp.sum(jnp.where(inside, places - starts[:, None], 0), axis=0)).astype(jnp.int32)
    right_room = lax.optimization_barrier(jnp.sum(jnp.where(inside, ends[:, None] - 1 - places, 0), axis=0)).astype(jnp.int32)
    return (left_room, right_room)

def taps(stream, dilation, left_room, right_room):
    row_count = stream.shape[1]
    padded = jnp.pad(stream, ((0, 0), (dilation, dilation)))
    before = padded[:, :row_count] * (left_room >= dilation).astype(stream.dtype)[None, :]
    after = padded[:, 2 * dilation:] * (right_room >= dilation).astype(stream.dtype)[None, :]
    return jnp.concatenate([before, stream, after], axis=0)

def flow_step(audio_part, mel_part, weights, left_room, right_room):
    lu_weight, start_weight, start_bias, in_weight, cond_weight, gate_bias, mix_weight, mix_bias, end_weight, end_bias = weights
    matrix = flow_matrix(lu_weight)
    mixed = jnp.dot(matrix, audio_part, precision=highest)
    front = mixed[:HALF]
    back = mixed[HALF:]
    stream = low_back(low(jnp.dot(start_weight, front, precision=highest) + start_bias[:, None]))
    skip_sum = jnp.zeros((SKIP, audio_part.shape[1]), jnp.float32)
    for layer_number in range(LAYERS):
        dilation = 2 ** layer_number
        stacked = taps(stream, dilation, left_room, right_room)
        pre_gate = jnp.dot(in_weight[layer_number], stacked, precision=highest)
        pre_gate = pre_gate + jnp.dot(cond_weight[layer_number], mel_part, precision=highest)
        pre_gate = low_back(pre_gate + gate_bias[layer_number][:, None])
        gated = low(jnp.tanh(pre_gate[:RES]) * jax.nn.sigmoid(pre_gate[RES:]))
        branch = jnp.dot(mix_weight[layer_number], gated, precision=highest) + mix_bias[layer_number][:, None]
        stream = low_back(low(stream + branch[:RES]))
        skip_sum = skip_sum + branch[RES:]
    ending = jnp.concatenate([stream, low(low_back(skip_sum))], axis=0)
    result = low_back(jnp.dot(end_weight, ending, precision=highest) + end_bias[:, None])
    log_scale = result[:HALF]
    shift_part = result[HALF:]
    coupled = jnp.exp(log_scale) * back + shift_part
    latent = jnp.concatenate([front, coupled], axis=0)
    logdet = lax.optimization_barrier(jnp.sum(log_scale, axis=0)) + jnp.trace(lu_weight)
    return (latent, logdet)

def reference(audio_in, mel_spec, lengths, z_cotangent, det_cotangent, lu_weight, start_weight, start_bias, in_weight, cond_weight, gate_bias, mix_weight, mix_bias, end_weight, end_bias):
    params = (lu_weight, start_weight, start_bias, in_weight.astype(jnp.float32), cond_weight.astype(jnp.float32), gate_bias, mix_weight.astype(jnp.float32), mix_bias, end_weight.astype(jnp.float32), end_bias)
    mel_full = mel_spec.astype(jnp.float32)
    row_count = MB_ROWS

    def one_block(totals, block):
        begin = block * row_count
        audio_block = lax.dynamic_slice_in_dim(audio_in, begin, row_count, 1)
        mel_block = lax.dynamic_slice_in_dim(mel_full, begin, row_count, 1)
        z_block = lax.dynamic_slice_in_dim(z_cotangent, begin, row_count, 1)
        det_block = lax.dynamic_slice_in_dim(det_cotangent, begin, row_count, 0)
        length_row = lax.dynamic_index_in_dim(lengths, block, 0, keepdims=False)
        left_room, right_room = rooms(length_row, row_count)

        def forward(audio_part, mel_part, weights):
            return flow_step(audio_part, mel_part, weights, left_room, right_room)
        outputs, pullback = jax.vjp(forward, audio_block, mel_block, params)
        audio_part_grad, mel_part_grad, weight_grads = pullback((z_block, det_block))
        totals = jax.tree.map(lambda running, addend: running + addend, totals, weight_grads)
        return (totals, (outputs[0], outputs[1], audio_part_grad, mel_part_grad))
    zeros = jax.tree.map(jnp.zeros_like, params)
    blocks = jnp.arange(lengths.shape[0], dtype=jnp.int32)
    totals, stacked = lax.scan(one_block, zeros, blocks)
    latent = jnp.moveaxis(stacked[0], 0, 1).reshape(GROUP, -1)
    logdet = stacked[1].reshape(-1)
    audio_grad = jnp.moveaxis(stacked[2], 0, 1).reshape(GROUP, -1)
    mel_grad = jnp.moveaxis(stacked[3], 0, 1).reshape(MEL, -1)
    return (latent, logdet, audio_grad, mel_grad, totals[0], totals[1], totals[2], totals[3], totals[4], totals[5], totals[6], totals[7], totals[8], totals[9])
```

```python
import functools

import jax
import jax.numpy as jnp
from jax import lax
from jax.experimental import pallas as pl
from jax.experimental.pallas import tpu as pltpu
from jax.sharding import PartitionSpec as P

BF = jnp.bfloat16
F32 = jnp.float32
LANES = 128
MISC = 48
MIB = 1 << 20
highest = lax.Precision.HIGHEST
VMEM = pltpu.VMEM
ANY = pl.ANY


def mm(first, second, first_dim=1, second_dim=0):
    return lax.dot_general(
        first, second, (((first_dim,), (second_dim,)), ((), ())), preferred_element_type=F32
    )


def split_high_low(values):
    high = values.astype(BF)
    return high, (values - high.astype(F32)).astype(BF)


def kept(rows, cols, dtype=BF):
    return pltpu.HBM((rows, cols), dtype)


def whole(space=VMEM):
    return pl.BlockSpec(memory_space=space)


def call(body, name, out_shape, scratch, grid=None, in_specs=None, out_specs=None, flops=0, nbytes=0, vmem=24):
    return pl.pallas_call(
        body,
        name=name,
        out_shape=out_shape,
        grid_spec=pltpu.PrefetchScalarGridSpec(
            num_scalar_prefetch=1,
            grid=grid or (1,),
            in_specs=in_specs,
            out_specs=out_specs,
            scratch_shapes=scratch,
        ),
        compiler_params=pltpu.CompilerParams(vmem_limit_bytes=vmem * MIB),
        cost_estimate=pl.CostEstimate(
            flops=int(flops), bytes_accessed=int(nbytes), transcendentals=0
        ),
    )


class Sizes:
    def __init__(self, args, cycle, data):
        (audio, mel, lengths, _, _, _, start_weight, _, in_weight, _, _, mix_weight) = args[:12]
        self.cycle, self.data = cycle, data
        self.micro, self.utts = lengths.shape
        self.copies = cycle // self.micro
        assert self.copies * self.micro == cycle
        self.frames = audio.shape[1] // self.micro
        self.group = audio.shape[0]
        self.half = self.group // 2
        self.mel = mel.shape[0]
        self.res = start_weight.shape[0]
        self.gate = in_weight.shape[1]
        self.taps = in_weight.shape[2]
        self.mixed_rows = mix_weight.shape[1]
        self.skip = self.mixed_rows - self.res
        self.ones = self.mel
        self.tap_rows = 3 * self.half + 2
        self.first = self.mel + 2
        self.x_rows = -(-(self.first + 3 * self.tap_rows) // LANES) * LANES
        self.all_rows = self.taps + self.x_rows
        self.pack_misc = self.res
        self.pack_cond = self.res + MISC
        self.me_rows = self.res + LANES
        self.cond_blocks = self.res // self.x_rows
        self.cond_rows = self.gate // self.cond_blocks
        self.pack_rows = self.pack_cond + self.cond_rows
        self.blocks = self.gate // LANES
        self.m_rows = self.mixed_rows // self.blocks
        self.m_fold = self.res // LANES
        self.m_pack = self.m_rows * self.m_fold
        self.share_first = self.x_rows + self.m_pack
        self.share_rows = self.taps + self.share_first
        self.direct = cycle == 4 and data == self.blocks
        self.bits = data.bit_length() - 1

    def tap(self, number):
        return self.first + number * self.tap_rows


def prepare_weights(z, in_w, cond, gate_bias, mix, mix_bias, start, end_w):
    def body(s_ref, in_ref, cond_ref, gb_ref, mix_ref, mb_ref, start_ref, end_ref, pack_ref, sx_ref, acc, in_v, sem):
        start_high, start_low = split_high_low(start_ref[...])
        start_pair = jnp.concatenate([start_high.astype(F32), start_low.astype(F32)], axis=0).astype(BF)
        in_copy = pltpu.make_async_copy(in_ref, in_v, sem)

        @pl.when(s_ref[0] == 0)
        def _():
            in_copy.start()

        col = lax.broadcasted_iota(jnp.int32, (8, z.x_rows), 1)

        row16 = lax.broadcasted_iota(jnp.int32, (16, z.x_rows), 0)
        col16 = lax.broadcasted_iota(jnp.int32, (16, z.x_rows), 1)

        def spread(tap):
            base, h = z.tap(tap), z.half
            spot = jnp.where(col16 < base + 3 * h, lax.rem(col16 - base + 3 * h, h), h)
            inside = (col16 >= base) & (col16 < base + z.tap_rows)
            hit = (inside & ((row16 & 7) == spot)).astype(F32).astype(BF)
            return mm(start_pair, hit, 0, 0)

        def is_low(tap):
            base = z.tap(tap)
            return ((col >= base + 2 * z.half) & (col < base + 3 * z.half)) | (col == base + 3 * z.half + 1)

        def choose(values, low_cols):
            high = values.astype(BF).astype(F32)
            return jnp.where(low_cols, values - high, high).astype(BF)

        eye = (
            lax.broadcasted_iota(jnp.int32, (z.mel, z.x_rows), 0)
            == lax.broadcasted_iota(jnp.int32, (z.mel, z.x_rows), 1)
        ).astype(F32).astype(BF)
        bias = gb_ref[...]
        bias_high = bias.astype(BF).astype(F32)
        bias_rows = jnp.concatenate([bias_high, bias - bias_high, jnp.zeros((14, z.gate), F32)], axis=0)
        pick = (((row16 == 0) & (col16 == z.ones)) | ((row16 == 1) & (col16 == z.ones + 1))).astype(F32)
        acc[...] = mm(cond_ref[...], eye) + mm(bias_rows.astype(BF), pick.astype(BF), 0, 0)
        middle = spread(1)
        end_res = end_ref[:, 0 : z.res]
        high, low = split_high_low(middle)
        ends_start = mm(end_res, high) + mm(end_res, low)
        sx_ref[0 : z.res, :] = choose(middle, is_low(1)[0:1, :])
        sx_ref[z.res :, :] = jnp.concatenate([choose(ends_start, is_low(1)).astype(F32), jnp.zeros((8, z.x_rows), F32)], axis=0).astype(BF)
        pack_ref[0 : z.res, :] = mix_ref[0 : z.res, :]
        ends = mm(end_ref[...], mix_ref[...])
        ends_high = ends.astype(BF).astype(F32)
        bias_end = jnp.sum(end_ref[...].astype(F32) * mb_ref[...], axis=1, keepdims=True)
        bias_end = jnp.broadcast_to(bias_end, (z.group, z.res))
        bias_end_high = bias_end.astype(BF).astype(F32)
        own = mb_ref[:, 0 : z.res]
        own_high = own.astype(BF).astype(F32)
        pack_ref[z.pack_misc : z.pack_misc + 16, :] = jnp.concatenate([ends_high, ends - ends_high], axis=0).astype(BF)
        pack_ref[z.pack_misc + 16 : z.pack_misc + 32, :] = jnp.concatenate(
            [bias_end_high, bias_end - bias_end_high], axis=0
        ).astype(BF)
        pack_ref[z.pack_misc + 32 : z.pack_misc + 48, :] = jnp.concatenate(
            [own_high, own - own_high, jnp.zeros((14, z.res), F32)], axis=0
        ).astype(BF)

        @pl.when(s_ref[0] == 0)
        def _():
            in_copy.wait()
            for tap in range(3):
                high, low = split_high_low(spread(tap))
                block = in_v[:, tap * z.res : (tap + 1) * z.res]
                acc[...] += mm(block, high) + mm(block, low)

        low_cols = (is_low(0) | is_low(1) | is_low(2))[0:1, :]
        cond_x = choose(acc[...], low_cols)
        for j in range(z.cond_blocks):
            pack_ref[z.pack_cond :, j * z.x_rows : (j + 1) * z.x_rows] = cond_x[
                j * z.cond_rows : (j + 1) * z.cond_rows
            ]

    return call(
        body,
        "prepare_weights",
        (
            kept(z.pack_rows, z.res),
            jax.ShapeDtypeStruct((z.res + 16, z.x_rows), BF),
        ),
        [pltpu.VMEM((z.gate, z.x_rows), F32), pltpu.VMEM((z.gate, z.taps), BF), pltpu.SemaphoreType.DMA],
        in_specs=[whole(ANY)] + [whole()] * 6,
        out_specs=(whole(), whole()),
        flops=2 * z.gate * z.taps * z.x_rows,
        nbytes=6 * MIB,
    )


def prepare_frames(z):
    def body(s_ref, len_ref, audio_ref, mel_ref, lu_ref, x_ref, mixed_ref, mask_ref, turned_ref, matrix_ref, tall):
        lu = lu_ref[...]
        r = lax.broadcasted_iota(jnp.int32, lu.shape, 0)
        c = lax.broadcasted_iota(jnp.int32, lu.shape, 1)
        lower = jnp.where(r > c, lu, 0.0) + jnp.where(r == c, 1.0, 0.0)
        upper = jnp.where(r < c, lu, 0.0) + jnp.where(r == c, jnp.exp(lu), 0.0)
        matrix = lower[:, 0:1] * upper[0:1, :]
        for k in range(1, z.group):
            matrix = matrix + lower[:, k : k + 1] * upper[k : k + 1, :]
        matrix_ref[...] = matrix
        mixed = matrix[:, 0:1] * audio_ref[0:1, :]
        for k in range(1, z.group):
            mixed = mixed + matrix[:, k : k + 1] * audio_ref[k : k + 1, :]
        mixed_ref[...] = mixed
        place = lax.broadcasted_iota(jnp.int32, (16, z.frames), 1)
        begin = jnp.int32(0)
        left = jnp.zeros((16, z.frames), jnp.int32)
        right = jnp.zeros((16, z.frames), jnp.int32)
        for u in range(z.utts):
            size = len_ref[s_ref[2], u]
            inside = (place >= begin) & (place < begin + size)
            left = jnp.where(inside, place - begin, left)
            right = jnp.where(inside, begin + size - 1 - place, right)
            begin = begin + size
        for l in range(z.cycle):
            mask_ref[l, 0:16, :] = (left >= 2**l).astype(F32).astype(BF)
            mask_ref[l, 16:32, :] = (right >= 2**l).astype(F32).astype(BF)
        tall[...] = jnp.zeros_like(tall)
        for l in range(z.cycle):
            tall[2 * l : 2 * l + 1, :] = (left >= 2**l).astype(F32)[0:1]
            tall[2 * l + 1 : 2 * l + 2, :] = (right >= 2**l).astype(F32)[0:1]
        turned_ref[...] = tall[...].T
        high = mixed.astype(BF).astype(F32)
        low = (mixed - high).astype(BF).astype(F32)
        tall[...] = jnp.zeros_like(tall)
        tall[0 : z.mel, :] = mel_ref[...].astype(F32)
        tall[z.ones : z.ones + 2, :] = jnp.ones((2, z.frames), F32)
        masks = ((left >= 1).astype(F32)[0:8], jnp.ones((8, z.frames), F32), (right >= 1).astype(F32)[0:8])
        for tap in range(3):
            shift = (1, 0, z.frames - 1)[tap]
            moved_high = (pltpu.roll(high, shift, axis=1) if shift else high) * masks[tap]
            moved_low = (pltpu.roll(low, shift, axis=1) if shift else low) * masks[tap]
            base = z.tap(tap)
            h = z.half
            tall[base : base + h, :] = moved_high[0:h]
            tall[base + h : base + 2 * h, :] = moved_low[0:h]
            tall[base + 2 * h : base + 3 * h, :] = moved_high[0:h]
            tall[base + 3 * h : base + 3 * h + 2, :] = masks[tap][0:2]
        x_ref[...] = tall[...].astype(BF)

    def column(rows):
        return pl.BlockSpec((rows, z.frames), lambda i, s: (0, s[2]))

    return call(
        body,
        "prepare_frames",
        (
            kept(z.x_rows, z.frames),
            jax.ShapeDtypeStruct((z.group, z.frames), F32),
            pltpu.HBM((z.cycle, 32, z.frames), BF),
            kept(z.frames, z.x_rows, F32),
            jax.ShapeDtypeStruct((z.group, z.group), F32),
        ),
        [pltpu.VMEM((z.x_rows, z.frames), F32)],
        in_specs=[whole(pltpu.SMEM), column(z.group), column(z.mel), whole()],
        out_specs=(whole(),) * 5,
        flops=1e6,
        nbytes=2 * MIB,
    )


def taps_copies(z, s_ref, sources, layer, target, sem):
    if len(sources) == 1:
        return [pltpu.make_async_copy(sources[0].at[layer], target, sem)], None
    copy = pltpu.make_async_copy
    if len(sources) == 4:
        return [[copy(source, target, sem)] for source in sources], s_ref[0] ^ layer
    own, near, far, beside, cross, cross_beside = sources
    rows = z.gate // 2
    x = s_ref[1] & 1
    mine = target.at[pl.ds(pl.multiple_of(x * rows, rows), rows)]
    other = target.at[pl.ds(pl.multiple_of((1 - x) * rows, rows), rows)]
    slots = [
        [copy(own, target, sem)],
        [copy(near, target, sem)],
        [copy(far, mine, sem), copy(beside, other, sem)],
        [copy(cross, mine, sem), copy(cross_beside, other, sem)],
    ]
    return slots, s_ref[0] ^ layer


def pack_copies(z, s_ref, packs, layer, me, wide, column, sems):
    def of(ref):
        conds = [
            pltpu.make_async_copy(
                ref.at[pl.ds(z.pack_cond, z.cond_rows), pl.ds(j * z.x_rows, z.x_rows)],
                wide.at[pl.ds(j * z.cond_rows, z.cond_rows), pl.ds(column, z.x_rows)],
                sems.at[0],
            )
            for j in range(z.cond_blocks)
        ]
        return conds + [
            pltpu.make_async_copy(ref.at[pl.ds(0, z.pack_cond)], me.at[pl.ds(0, z.pack_cond)], sems.at[1])
        ]

    if len(packs) == 1:
        return of(packs[0].at[layer]), None
    return [of(ref) for ref in packs], s_ref[0] ^ layer


def each(copies, action):
    chosen, slot = copies
    if slot is None:
        for copy in chosen:
            getattr(copy, action)()
        return
    for number, group in enumerate(chosen):

        @pl.when(slot == number)
        def _():
            for copy in group:
                getattr(copy, action)()


def fill_taps(z, taps, mask, layer):
    dilation = 2**layer
    rows = 32

    def one(i, _):
        begin = pl.multiple_of(i * rows, rows)
        block = taps[pl.ds(z.res + begin, rows), :]
        before = pltpu.roll(block, dilation, axis=1).reshape(rows // 16, 16, z.frames)
        after = pltpu.roll(block, z.frames - dilation, axis=1).reshape(rows // 16, 16, z.frames)
        taps[pl.ds(begin, rows), :] = (before * mask[0:16, :][None]).reshape(rows, z.frames)
        taps[pl.ds(2 * z.res + begin, rows), :] = (after * mask[16:32, :][None]).reshape(rows, z.frames)
        return 0

    lax.fori_loop(0, z.res // rows, one, 0)


class Copies:
    def __init__(self, sems):
        self.sems, self.used = sems, 0

    def start(self, source, target):
        copy = pltpu.make_async_copy(source, target, self.sems.at[self.used])
        self.used += 1
        copy.start()
        return copy

    def weights(self, z, s_ref, sources, packs, layer, wide, me, column):
        pack = pack_copies(z, s_ref, packs, layer, me, wide, column, self.sems.at[pl.ds(self.used, 2)])
        self.used += 2
        each(pack, "start")
        if not layer:
            return pack, None
        taps = taps_copies(z, s_ref, sources, layer, wide.at[:, pl.ds(0, z.taps)], self.sems.at[self.used])
        self.used += 1
        each(taps, "start")
        return pack, taps


def gate_parts(first, second):
    tanh = jnp.tanh(first)
    sig = 0.5 * jnp.tanh(0.5 * second) + 0.5
    gated = tanh * sig
    return gated.astype(BF), (sig - gated * tanh).astype(BF), (gated - gated * sig).astype(BF)


def bias_column(z, me):
    row = lax.broadcasted_iota(jnp.int32, (16, LANES), 0)
    pick = (row < 2).astype(F32).astype(BF)
    return mm(me[z.pack_misc + 32 : z.pack_misc + 48, :], pick, 0, 0)[:, 0:1]


def bias_end(z, me):
    rows = me[z.pack_misc + 16 : z.pack_misc + 32, :].astype(F32)
    return (rows[0 : z.group] + rows[z.group : 2 * z.group])[:, 0:1]


def forward_parts(z, layer, wide, taps, me, pre, add_end, start_of, save, gated_v, fa_v, fb_v, out_v, total):
    width = pre.shape[2]
    parts = z.frames // width
    mix_rows = 0 if layer == z.cycle - 1 else z.res
    add_stream = bias_column(z, me) if mix_rows else None

    def product(part):
        pre[part % 2, :, :] = mm(wide[...], taps[:, part * width : (part + 1) * width])

    product(0)
    for part in range(parts):
        if part + 1 < parts:
            product(part + 1)
        here = slice(part * width, (part + 1) * width)
        gated, fa, fb = gate_parts(pre[part % 2, 0 : z.res, :], pre[part % 2, z.res :, :])
        gated_v[:, here] = gated
        fa_v[here, :] = fa.T
        fb_v[here, :] = fb.T
        branch = mm(me[z.res - mix_rows : z.res + 16, :], gated)
        ends = branch[mix_rows : mix_rows + z.group] + branch[mix_rows + z.group :] + add_end
        if start_of is None:
            total[:, here] = total[:, here] + ends
        else:
            start = start_of(here)
            total[:, here] = ends + start[z.res : z.res + z.group]
        if mix_rows:
            stream = taps[z.res : 2 * z.res, here].astype(F32) if start_of is None else start[0 : z.res]
            if start_of is not None:
                stream = stream.astype(BF).astype(F32)
            out_v[:, here] = (stream + branch[0 : z.res] + add_stream).astype(BF)
        save(part)


def forward_group(z, n_sources, n_packs):
    width = 256
    parts = z.frames // width
    count = z.cycle - 1

    def body(s_ref, *refs):
        refs = list(refs)
        take = lambda n: [refs.pop(0) for _ in range(n)]
        sources, packs = take(n_sources), take(n_packs)
        (x_ref, mask_ref, sx_ref) = take(3)
        kept_refs = [take(4) for _ in range(count)]
        (total,) = take(1)
        (wides, first_wide, all_taps, x_v, mes, pre, gated_vs, fa_vs, fb_vs, masks, sems) = take(11)
        copies = Copies(sems)
        pending = {0: copies.weights(z, s_ref, sources, packs, 0, first_wide, mes.at[0], 0)}
        x_in = copies.start(x_ref, x_v)
        mask_in = copies.start(mask_ref, masks)
        x_taps = [copies.start(x_ref, all_taps.at[k, pl.ds(z.taps, z.x_rows)]) for k in range(2)]

        def bring(layer):
            k = layer % 2
            pending[layer] = copies.weights(z, s_ref, sources, packs, layer, wides.at[k], mes.at[k], z.taps)

        if count > 1:
            bring(1)
        x_in.wait()
        saves = {}
        for layer in range(count):
            k = layer % 2
            pack, taps_in = pending[layer]
            if layer and layer + 1 < count:
                bring(layer + 1)
            me = mes.at[k]
            taps = all_taps.at[k] if layer else x_v
            wide = wides.at[k] if layer else first_wide
            if layer == 1:
                mask_in.wait()
                for copy in x_taps:
                    copy.wait()
            if layer:
                fill_taps(z, taps, masks.at[layer], layer)
            each(pack, "wait")
            if layer:
                each(taps_in, "wait")
            for done in (layer - 1, layer - 2):
                for copy in saves.pop(done, []):
                    copy.wait()
            gated_v, fa_v, fb_v = gated_vs.at[k], fa_vs.at[k], fb_vs.at[k]
            out_v = all_taps.at[1 - k, pl.ds(z.res, z.res)]
            gated_ref, fa_ref, fb_ref, out_ref = kept_refs[layer]
            mine = saves[layer] = []

            def save(part):
                at = pl.ds(part * width, width)
                mine.append(copies.start(gated_v.at[:, at], gated_ref.at[:, at]))
                mine.append(copies.start(fa_v.at[at], fa_ref.at[at]))
                mine.append(copies.start(fb_v.at[at], fb_ref.at[at]))
                mine.append(copies.start(out_v.at[:, at], out_ref.at[:, at]))

            start_of = None if layer else (lambda here: mm(sx_ref[...], x_v[:, here]))
            forward_parts(
                z, layer, wide, taps, me, pre, bias_end(z, me), start_of, save, gated_v, fa_v, fb_v, out_v, total
            )
        for group in saves.values():
            for copy in group:
                copy.wait()
        if count == 1:
            mask_in.wait()
            for copy in x_taps:
                copy.wait()

    outs, out_specs = [], []
    for _ in range(count):
        outs += [kept(z.res, z.frames), kept(z.frames, z.res), kept(z.frames, z.res), kept(z.res, z.frames)]
        out_specs += [whole(ANY)] * 4
    outs.append(jax.ShapeDtypeStruct((z.group, z.frames), F32))
    out_specs.append(whole())
    return call(
        body,
        "forward_group",
        tuple(outs),
        [
            pltpu.VMEM((2, z.gate, z.all_rows), BF),
            pltpu.VMEM((z.gate, z.x_rows), BF),
            pltpu.VMEM((2, z.all_rows, z.frames), BF),
            pltpu.VMEM((z.x_rows, z.frames), BF),
            pltpu.VMEM((2, z.me_rows, z.res), BF),
            pltpu.VMEM((2, z.gate, width), F32),
            pltpu.VMEM((2, z.res, z.frames), BF),
            pltpu.VMEM((2, z.frames, z.res), BF),
            pltpu.VMEM((2, z.frames, z.res), BF),
            pltpu.VMEM((z.cycle, 32, z.frames), BF),
            pltpu.SemaphoreType.DMA((8 + count * (4 * parts + 3),)),
        ],
        in_specs=[whole(ANY)] * (n_sources + n_packs + 2) + [whole()],
        out_specs=tuple(out_specs),
        flops=8 * count * z.frames * z.gate * z.taps,
        nbytes=40 * MIB,
        vmem=50,
    )


def gradient_group(z, high, n_after, n_high, n_low, n_packs):
    low = high - 1
    last, first = high == z.cycle - 1, low == 0
    width = 256
    shares = z.blocks // 2
    half_rows = z.share_rows // 2
    extra = z.share_first // 2 if first else 0

    def body(s_ref, *refs):
        refs = list(refs)
        take = lambda n: [refs.pop(0) for _ in range(n)]
        take(n_after)
        sources = {high: take(n_high), low: take(n_low)}
        packs = take(n_packs)
        (x_ref, mask_ref, end_ref, stream_high) = take(4)
        if last:
            (res_ref, zcot_ref, cot_det_ref, mixed_ref, endb_ref, lu_ref) = take(6)
            other_gated = take(z.cycle - 2)
        else:
            (dres_in, h_in, dx_in) = take(3)
            saved_high = take(3)
        saved_low = take(3)
        if first:
            (turned_in, sx_ref, base_ref, matrix_ref, audio_ref, lu_ref, det_ref) = take(7)
        else:
            (stream_low, turned_in) = take(2)
        (stay_ref, cross_ref) = take(2)
        if first:
            (tail_ref, mel_ref, agrad_ref) = take(3)
        else:
            (h_out, dx_out) = take(2)
        if last:
            (p_ref, a_ref, latent_ref, logdet_ref, dres_out, base_out) = take(6)
        (wides, mes, all_taps, gated_vs, fa_vs, fb_vs, dpre, grads, hs, dx_ref, turned, dres_ref, masks, sems) = take(14)
        if last:
            (pre, total, spare) = take(3)
        if first:
            (low_wide, low_grads, in_v) = take(3)
        copies = Copies(sems)

        mask_in = copies.start(mask_ref, masks)
        high_in = [copies.start(stream_high, all_taps.at[0, pl.ds(z.res, z.res)])]
        if not last:
            gate_in = [copies.start(dres_in, dres_ref)]
        pack_high, taps_high = copies.weights(
            z, s_ref, sources[high], packs, high, wides.at[0], mes.at[0], z.taps
        )
        x_in = [copies.start(x_ref, all_taps.at[0, pl.ds(z.taps, z.x_rows)])]
        if not last:
            gate_in += [copies.start(h_in, hs.at[0])]
            gate_in += [copies.start(a, b.at[0]) for a, b in zip(saved_high[1:], (fa_vs, fb_vs))]
            mix_in = [copies.start(saved_high[0], gated_vs.at[0]), copies.start(dx_in, dx_ref)]
        else:
            mix_in = [copies.start(a, spare.at[i]) for i, a in enumerate(other_gated[:2])]
        turned_copy = copies.start(turned_in, turned)
        low_k = 0 if first else 1
        if first:
            in_copies = taps_copies(z, s_ref, sources[0], 0, in_v, sems.at[copies.used])
            copies.used += 1
            low_x = all_taps.at[0, pl.ds(z.taps, z.x_rows)]
            pack_low, taps_low = copies.weights(z, s_ref, None, packs, 0, low_wide, mes.at[1], 0)
            each(in_copies, "start")
            low_in = []
        else:
            low_x = all_taps.at[1, pl.ds(z.taps, z.x_rows)]
            low_in = [copies.start(stream_low, all_taps.at[1, pl.ds(z.res, z.res)])]
            pack_low, taps_low = copies.weights(
                z, s_ref, sources[low], packs, low, wides.at[1], mes.at[1], z.taps
            )
            x_in.append(copies.start(x_ref, low_x))
        gate_low = [copies.start(a, b.at[1]) for a, b in zip(saved_low[1:], (fa_vs, fb_vs))]
        mix_low = copies.start(saved_low[0], gated_vs.at[1])

        for k in range(2):
            mes[k, z.pack_cond :, :] = jnp.zeros((z.me_rows - z.pack_cond, z.res), BF)
        mask_in.wait()
        for copy in high_in:
            copy.wait()
        fill_taps(z, all_taps.at[0], masks.at[high], high)
        for copy in x_in:
            copy.wait()
        each(pack_high, "wait")
        if last:
            each(taps_high, "wait")
            lu = lu_ref[...]
            r = lax.broadcasted_iota(jnp.int32, lu.shape, 0)
            c = lax.broadcasted_iota(jnp.int32, lu.shape, 1)
            trace = jnp.sum(jnp.where(r == c, lu, 0.0))
            total[...] = res_ref[...]
            forward_parts(
                z, high, wides.at[0], all_taps.at[0], mes.at[0], pre, bias_end(z, mes.at[0]) + endb_ref[...],
                None, lambda part: None, gated_vs.at[0], fa_vs.at[0], fb_vs.at[0], None, total,
            )
            h = z.half
            is_scale = lax.broadcasted_iota(jnp.int32, (z.group, z.frames), 0) < h
            turn = lambda rows: pltpu.roll(rows, h, axis=0)
            ends = total[...]
            growth = jnp.where(is_scale, jnp.exp(jnp.where(is_scale, ends, 0.0)), 0.0)
            mixed, zcot = mixed_ref[...], zcot_ref[...]
            grown = growth * turn(mixed)
            latent_ref[...] = jnp.where(is_scale, mixed, turn(grown) + ends)
            logdet_ref[...] = jnp.sum(jnp.where(is_scale, ends, 0.0), axis=0, keepdims=True) + trace
            dres = jnp.where(is_scale, turn(zcot) * grown + cot_det_ref[...], zcot)
            dres = jnp.concatenate([dres, dres, jnp.zeros((LANES - 16, z.frames), F32)], axis=0)
            dres_ref[...] = dres.T.astype(BF)
            base_out[...] = zcot * jnp.where(is_scale, 1.0, turn(growth))
            leaving = [copies.start(dres_ref, dres_out)]
        else:
            for copy in gate_in:
                copy.wait()
            leaving = []

        two = lambda exact: jnp.concatenate(
            [exact.astype(BF).astype(F32), exact - exact.astype(BF).astype(F32)], axis=0
        ).astype(BF)
        dsum = jnp.sum(dres_ref[...].astype(F32), axis=0, keepdims=True)
        end_bias = mm(two(jnp.concatenate([dsum, jnp.zeros((7, LANES), F32)], axis=0)), end_ref[16:, :])
        end_bias = end_bias[0:8] + end_bias[8:16]

        def gate_and_mix(layer, k, h_ref, grad_rows, at, ready):
            me = mes.at[k]
            for n in range(z.res // width):
                cols = slice(n * width, (n + 1) * width)
                dgated = mm(dres_ref[...], me[z.res :, cols])
                if h_ref is not None:
                    dgated = dgated + mm(h_ref[...], me[0 : z.res, cols])
                dpre[:, cols] = (dgated * fa_vs[k, :, cols].astype(F32)).astype(BF)
                dpre[:, z.res + n * width : z.res + (n + 1) * width] = (
                    dgated * fb_vs[k, :, cols].astype(F32)
                ).astype(BF)
            for copy in ready:
                copy.wait()
            outer = mm(gated_vs[k], dres_ref[...]).T[0 : z.group]
            mix_grad = mm(end_ref[0:16, :], two(outer), 0, 0)
            bias_grad = end_bias
            if h_ref is not None:
                h_mix = mm(gated_vs[k], h_ref[...]).T
                mix_grad = mix_grad + jnp.concatenate([h_mix, jnp.zeros((z.skip, z.res), F32)], axis=0)
                h_sum = jnp.sum(h_ref[...].astype(F32), axis=0, keepdims=True)
                h_sum = jnp.concatenate([h_sum, jnp.zeros((7, z.res), F32)], axis=0)
                bias_grad = bias_grad + jnp.concatenate([h_sum, jnp.zeros((8, z.skip), F32)], axis=1)
            mix_grad = mix_grad.astype(BF)
            for s in range(z.blocks):
                for j in range(z.m_fold):
                    top = at + j * z.m_rows
                    grad_rows[s, top : top + z.m_rows, :] = mix_grad[
                        s * z.m_rows : (s + 1) * z.m_rows, j * LANES : (j + 1) * LANES
                    ]
            return outer, bias_grad

        row = lax.broadcasted_iota(jnp.int32, (z.x_rows, LANES), 0)

        def with_bias(block, bias_grad, s):
            moved = pltpu.roll(bias_grad, (z.mixed_rows - s * z.m_rows) % z.mixed_rows, axis=1) if s else bias_grad
            return jnp.where(row == z.x_rows - 1, moved[0:1, 0:LANES], block).astype(BF)

        def taps_gradients(k, bias_grad):
            for n in range(z.gate // width):
                part = mm(all_taps[k], dpre[:, n * width : (n + 1) * width])
                for i in range(width // LANES):
                    s = n * (width // LANES) + i
                    lanes = slice(i * LANES, (i + 1) * LANES)
                    grads[s, 0 : z.taps, :] = part[0 : z.taps, lanes].astype(BF)
                    grads[s, z.taps : z.taps + z.x_rows, :] = with_bias(part[z.taps :, lanes], bias_grad, s)

        sent_sem = sems.at[copies.used]
        copies.used += 1

        def send(layer, grad_rows, rows, top):
            owner = max(layer, 1)
            away = (s_ref[0] ^ owner) & 1
            off_side = ((s_ref[0] ^ owner) >> 1) & 1
            for s in range(z.blocks):
                for half in range(2):
                    if z.direct:
                        v = s_ref[1] ^ s
                        place = (off_side ^ half) << (z.bits - 1)
                        for b in range(1, z.bits):
                            place = place | (((v >> b) & 1) << (z.bits - 1 - b))
                        to_stay = (v & 1) == away
                        role = away
                    else:
                        place, to_stay = jnp.int32((s % shares) * 2 + half), jnp.int32(s) < shares
                        role = jnp.int32(high - layer)
                    block = grad_rows.at[s, pl.ds(half * rows, rows)]
                    if first:
                        stay_at = stay_ref.at[place, pl.ds(top, rows)]
                        cross_at = cross_ref.at[place, pl.ds(top, rows)]
                    else:
                        stay_at = stay_ref.at[role, place]
                        cross_at = cross_ref.at[1 - role if z.direct else role, place]

                    @pl.when(to_stay)
                    def _():
                        pltpu.make_async_copy(block, stay_at, sent_sem).start()

                    @pl.when(jnp.logical_not(to_stay))
                    def _():
                        pltpu.make_async_copy(block, cross_at, sent_sem).start()

        def sent_wait(grad_rows, rows):
            target = stay_ref.at[0, pl.ds(0, rows)] if first else stay_ref.at[0, 0]
            for _ in range(2 * z.blocks):
                pltpu.make_async_copy(grad_rows.at[0, pl.ds(0, rows)], target, sent_sem).wait()

        def stream_gradient(layer, k, h_ref, new_h):
            d = 2**layer
            dx = mm(dpre[...], wides[k, :, z.taps :])
            dx_ref[...] = dx if layer == z.cycle - 1 else dx + dx_ref[...]
            keep_before = turned[:, 2 * layer : 2 * layer + 1]
            keep_after = turned[:, 2 * layer + 1 : 2 * layer + 2]
            for n in range(z.res // width):
                cols = slice(n * width, (n + 1) * width)
                side = [
                    mm(dpre[...], wides[k, :, i * z.res + n * width : i * z.res + (n + 1) * width]) for i in range(3)
                ]
                result = side[1] + pltpu.roll(side[0] * keep_before, z.frames - d, axis=0)
                result = result + pltpu.roll(side[2] * keep_after, d, axis=0)
                if h_ref is not None:
                    result = result + h_ref[:, cols].astype(F32)
                new_h[:, cols] = result.astype(BF)

        h_high = None if last else hs.at[0]
        outer, bias_grad = gate_and_mix(high, 0, h_high, grads, z.taps + z.x_rows, [] if last else mix_in)
        if last:
            p_ref[high, :, :] = outer
            a_ref[...] = mm(all_taps[0, z.taps :, :], dres_ref[...]).T[0 : z.group]
            for i in range(z.cycle - 2):
                mix_in[i].wait()
                p_ref[i, :, :] = mm(spare[i % 2], dres_ref[...]).T[0 : z.group]
                if i + 2 < z.cycle - 2:
                    mix_in.append(copies.start(other_gated[i + 2], spare.at[i % 2]))
        taps_gradients(0, bias_grad)
        send(high, grads, half_rows, 0)
        turned_copy.wait()
        if not last:
            each(taps_high, "wait")
        stream_gradient(high, 0, h_high, hs.at[1])
        for copy in low_in:
            copy.wait()
        if not first:
            fill_taps(z, all_taps.at[1], masks.at[low], low)
        each(pack_low, "wait")
        for copy in gate_low:
            copy.wait()
        sent_wait(grads, half_rows)
        if not first:
            outer, bias_grad = gate_and_mix(low, 1, hs.at[1], grads, z.taps + z.x_rows, [mix_low])
            if last:
                p_ref[low, :, :] = outer
            taps_gradients(1, bias_grad)
            send(low, grads, half_rows, 0)
            each(taps_low, "wait")
            stream_gradient(low, 1, hs.at[1], hs.at[0])
            leaving += [copies.start(hs.at[0], h_out), copies.start(dx_ref, dx_out)]
            sent_wait(grads, half_rows)
        else:
            outer, bias_grad = gate_and_mix(0, 1, hs.at[1], low_grads, z.x_rows, [mix_low])
            dcond = mm(low_x[...], dpre[...])
            for s in range(z.blocks):
                low_grads[s, 0 : z.x_rows, :] = with_bias(dcond[:, s * LANES : (s + 1) * LANES], bias_grad, s)
            send(0, low_grads, extra, half_rows)
            h = z.half
            g_first = hs.at[0]
            g_first[...] = (hs[1].astype(F32) + mm(dres_ref[...], end_ref[16:, 0 : z.res])).astype(BF)
            dx = dx_ref[...] + mm(dpre[...], low_wide[...]) + mm(g_first[...], sx_ref[0 : z.res, :])
            dx = dx.T
            hx = mm(low_x[...], g_first[...])

            def folded(rows, tap):
                base = z.tap(tap)
                return [rows[base : base + h] + rows[base + h : base + 2 * h], rows[base + 3 * h : base + 3 * h + 1]]

            q = jnp.concatenate(
                folded(dcond, 0) + folded(dcond, 1) + folded(dcond, 2) + [jnp.zeros((16 - 3 * (h + 1), z.gate), F32)],
                axis=0,
            )
            each(in_copies, "wait")
            back = mm(two(q), in_v[...])
            start_rows = jnp.concatenate(folded(hx, 1), axis=0)
            for tap in range(3):
                top = tap * (h + 1)
                part = back[:, tap * z.res : (tap + 1) * z.res]
                start_rows = start_rows + part[top : top + h + 1] + part[16 + top : 16 + top + h + 1]
            tail_ref[...] = jnp.zeros_like(tail_ref)
            tail_ref[0 : h + 1, :] = start_rows
            mel_ref[...] = dx[0 : z.mel, :]
            keep_before = masks[0, 0:16, :].astype(F32)[0:h]
            keep_after = masks[0, 16:32, :].astype(F32)[0:h]
            tap_rows = []
            for tap in range(3):
                base = z.tap(tap)
                tap_rows.append(dx[base : base + h, :] + dx[base + 2 * h : base + 3 * h, :])
            zero = jnp.zeros((8 - h, z.frames), F32)
            pad = lambda v: jnp.concatenate([v, zero], axis=0)
            front = pad(tap_rows[1])
            front = front + pltpu.roll(pad(tap_rows[0] * keep_before), z.frames - 1, axis=1)
            front = front + pltpu.roll(pad(tap_rows[2] * keep_after), 1, axis=1)
            dmixed = front + base_ref[...]
            matrix = matrix_ref[...]
            r = lax.broadcasted_iota(jnp.int32, matrix.shape, 0)
            c = lax.broadcasted_iota(jnp.int32, matrix.shape, 1)
            flipped = matrix.T
            agrad = jnp.zeros((z.group, z.frames), F32)
            for k in range(z.group):
                agrad = agrad + flipped[:, k : k + 1] * dmixed[k : k + 1, :]
            agrad_ref[...] = agrad
            dmatrix = jnp.zeros((z.group, z.group), F32)
            for k in range(z.group):
                column = jnp.sum(dmixed * audio_ref[k : k + 1, :], axis=1, keepdims=True)
                dmatrix = dmatrix + jnp.where(c == k, column, 0.0)
            lu = lu_ref[...]
            lower = jnp.where(r > c, lu, 0.0) + jnp.where(r == c, 1.0, 0.0)
            grown = jnp.where(r == c, jnp.exp(lu), 0.0)
            upper = jnp.where(r < c, lu, 0.0) + grown
            upper_t = upper.T
            lower_t = lower.T
            dlower = jnp.zeros_like(lu)
            dupper = jnp.zeros_like(lu)
            for k in range(z.group):
                dlower = dlower + dmatrix[:, k : k + 1] * upper_t[k : k + 1, :]
                dupper = dupper + lower_t[:, k : k + 1] * dmatrix[k : k + 1, :]
            total_lu = jnp.where(r > c, dlower, 0.0) + jnp.where(r < c, dupper, 0.0) + dupper * grown
            tail_ref[8 : 8 + z.group, 0 : z.group] = total_lu + jnp.where(r == c, jnp.sum(det_ref[...]), 0.0)
            tail_ref[8:9, LANES : 2 * LANES] = dsum
            sent_wait(low_grads, extra)
        for copy in leaving:
            copy.wait()

    def column(rows):
        return pl.BlockSpec((rows, z.frames), lambda i, s: (0, s[2]))

    in_specs = [whole(ANY)] * (n_after + n_high + n_low + n_packs + 2) + [whole(), whole(ANY)]
    if last:
        in_specs += [whole(), column(z.group), column(1), whole(), whole(), whole()] + [whole(ANY)] * (z.cycle - 2)
    else:
        in_specs += [whole(ANY)] * 6
    in_specs += [whole(ANY)] * 3
    if first:
        in_specs += [whole(ANY), whole(), whole(), whole(), column(z.group), whole(), column(1)]
    else:
        in_specs += [whole(ANY)] * 2
    lead = () if first else (2,)
    outs = [pltpu.HBM((*lead, 2 * shares, half_rows + extra, LANES), BF)] * 2
    out_specs = [whole(ANY)] * 2
    if first:
        outs += [
            jax.ShapeDtypeStruct((16, z.res), F32),
            jax.ShapeDtypeStruct((z.mel, z.frames), F32),
            jax.ShapeDtypeStruct((z.group, z.frames), F32),
        ]
        out_specs += [whole()] * 3
    else:
        outs += [kept(z.frames, z.res), kept(z.frames, z.x_rows, F32)]
        out_specs += [whole(ANY)] * 2
    if last:
        outs += [
            jax.ShapeDtypeStruct((z.cycle, z.group, z.res), F32),
            jax.ShapeDtypeStruct((z.group, z.x_rows), F32),
            jax.ShapeDtypeStruct((z.group, z.frames), F32),
            jax.ShapeDtypeStruct((1, z.frames), F32),
            kept(z.frames, LANES),
            jax.ShapeDtypeStruct((z.group, z.frames), F32),
        ]
        out_specs += [whole()] * 4 + [whole(ANY), whole()]
    sets = 1 if first else 2
    scratch = [
        pltpu.VMEM((sets, z.gate, z.all_rows), BF),
        pltpu.VMEM((2, z.me_rows, z.res), BF),
        pltpu.VMEM((sets, z.all_rows, z.frames), BF),
        pltpu.VMEM((2, z.res, z.frames), BF),
        pltpu.VMEM((2, z.frames, z.res), BF),
        pltpu.VMEM((2, z.frames, z.res), BF),
        pltpu.VMEM((z.frames, z.gate), BF),
        pltpu.VMEM((z.blocks, z.share_rows, LANES), BF),
        pltpu.VMEM((2, z.frames, z.res), BF),
        pltpu.VMEM((z.frames, z.x_rows), F32),
        pltpu.VMEM((z.frames, z.x_rows), F32),
        pltpu.VMEM((z.frames, LANES), BF),
        pltpu.VMEM((z.cycle, 32, z.frames), BF),
        pltpu.SemaphoreType.DMA((40,)),
    ]
    if last:
        scratch += [
            pltpu.VMEM((2, z.gate, width), F32),
            pltpu.VMEM((z.group, z.frames), F32),
            pltpu.VMEM((2, z.res, z.frames), BF),
        ]
    if first:
        scratch += [
            pltpu.VMEM((z.gate, z.x_rows), BF),
            pltpu.VMEM((z.blocks, z.share_first, LANES), BF),
            pltpu.VMEM((z.gate, z.taps), BF),
        ]
    return call(
        body,
        "gradient_first" if first else "gradient_last" if last else "gradient_group",
        tuple(outs),
        scratch,
        in_specs=in_specs,
        out_specs=tuple(out_specs),
        flops=(60 if last else 40) * z.frames * z.gate * z.taps,
        nbytes=20 * MIB,
        vmem=58,
    )


def finish(z):
    def body(s_ref, own_ref, mix_ref, mb_ref, st_ref, a_ref, out_ref):
        h = z.half
        outer = own_ref[0 : z.group, :]
        high = outer.astype(BF).astype(F32)
        ends = mm(jnp.concatenate([high, outer - high], axis=0).astype(BF), mix_ref[...], 1, 1)
        ends = ends[0 : z.group] + ends[z.group :] + own_ref[8 : 8 + z.group, 0:1] * mb_ref[...]
        base = z.tap(1)
        a = a_ref[...]
        front = jnp.zeros((z.group, z.res), F32)
        for j in range(h + 1):
            if j < h:
                column = a[:, base + j : base + j + 1] + a[:, base + h + j : base + h + j + 1]
            else:
                column = a[:, base + 3 * h : base + 3 * h + 1]
            front = front + column * st_ref[j : j + 1, :]
        out_ref[0:8, :] = ends[:, 0 : z.res] + front
        out_ref[8:16, :] = jnp.zeros((8, z.res), F32)
        out_ref[8:16, 0 : z.skip] = ends[:, z.res :]

    return call(
        body,
        "finish",
        jax.ShapeDtypeStruct((16, z.res), F32),
        [],
        in_specs=[whole()] * 5,
        out_specs=whole(),
        flops=1e7,
        nbytes=MIB,
    )


def permute(z, block, move):
    pairs = []
    for dp in range(z.data):
        for li in range(z.cycle):
            to = move(dp, li)
            if to is not None:
                pairs.append((dp * z.cycle + li, to[0] * z.cycle + to[1]))
    return lax.ppermute(block, ("dp", "layer"), pairs)


def in_hbm(arrays):
    return [pltpu.with_memory_space_constraint(array, pltpu.HBM) for array in arrays]


def tie(value, *earlier):
    return lax.optimization_barrier((value, *earlier))[0]


def near_weights(z, in_w, group_place, prepared):
    if z.cycle != 4:
        ready = prepared()
        gathered = lax.all_gather(in_w, "layer")
        return ready, layer_packs(z, ready[0]), [gathered], gathered
    rows = z.gate // 2
    part = lax.dynamic_slice_in_dim(in_w, (group_place & 1) * rows, rows, 0)
    far = permute(z, part, lambda dp, li: (dp, li ^ 2) if li in (1, 2) else None)
    near = permute(z, in_w, lambda dp, li: (dp, li ^ 1))
    ready = prepared()
    packs = layer_packs(z, ready[0])
    far = tie(far, ready[1], packs[1])
    beside = permute(z, far, lambda dp, li: (dp ^ 1, li) if li in (3, 0) else None)
    far_late = permute(z, tie(in_w, far, packs[2]), lambda dp, li: (dp, li ^ 2) if li in (3, 0) else None)
    across = lambda dp, li: (dp, li ^ 1) if li in (3, 0) else None
    cross, cross_beside = permute(z, far, across), permute(z, beside, across)
    return ready, packs, [in_w, near, far, beside, cross, cross_beside], far_late


def late_weights(z, sources, far, token):
    if z.cycle != 4:
        return sources
    far = tie(far, token)
    return [*sources[:2], far, permute(z, far, lambda dp, li: (dp, li ^ 1) if li in (1, 2) else None)]


def layer_packs(z, pack):
    if z.cycle != 4:
        return [lax.all_gather(pack, "layer")]
    near = permute(z, pack, lambda dp, li: (dp, li ^ 1))
    far = permute(z, pack, lambda dp, li: (dp, li ^ 2))
    cross = permute(z, far, lambda dp, li: (dp, li ^ 1))
    return [pack, near, far, cross]


def add(*terms):
    total = terms[0].astype(F32)
    for term in terms[1:]:
        total = total + term.astype(F32)
    return total


def sent(z, blocks, *moves):
    many = isinstance(blocks, list)
    blocks = blocks if many else [blocks]
    got = yield blocks, [permute(z, block, move) for block, move in zip(blocks, moves)]
    return got if many else got[0]


def meet_core(z, stay, cross):
    got = yield from sent(z, cross, lambda dp, li: (dp, li ^ 1))
    count = z.data // 2
    if stay.ndim == 3:
        stay, got = stay[None], got[None]
    near = [add(stay[role, :count], got[role, :count]).astype(BF) for role in range(stay.shape[0])]
    far = [add(stay[role, count:], got[role, count:]).astype(BF) for role in range(stay.shape[0])]
    return near, far


def reduce_chips(z, side, at_home, operands):
    near, far, near_other, far_other = operands
    count = z.data // 2
    away = (lambda li: not at_home(li)) if near is near_other else at_home
    by_y, by_x, by_both = yield from sent(
        z,
        [far, near_other, far_other],
        lambda dp, li: (dp, li ^ 2) if at_home(li) else None,
        lambda dp, li: (dp ^ 1, li ^ 1) if away(li) else None,
        lambda dp, li: (dp ^ 1, li ^ 3) if away(li) else None,
    )
    parts = [near, by_y, by_x, by_both]
    for b in range(1, z.bits):
        count //= 2
        send = add(*(part[count:] for part in parts)).astype(BF)
        keep = add(*(part[:count] for part in parts)).astype(BF)
        got = yield from sent(z, send, lambda dp, li: (dp ^ (1 << b), li) if at_home(li) else None)
        parts = [keep, got]
    total = add(keep[0], got[0])
    got = yield from sent(
        z, total.astype(BF), lambda dp, li: (dp, li ^ 2) if at_home(li) and (li & 2) != side else None
    )
    return total, got.astype(F32)


def reduce_last_two(z, stay, cross):
    near, far = yield from meet_core(z, stay, cross)
    operands = (near[0], far[0], near[1], far[1])
    total, got = yield from reduce_chips(z, 2, lambda li: True, operands)
    return jnp.concatenate([total, got], axis=0)


def reduce_first_two(z, stay, cross):
    near, far = yield from meet_core(z, stay, cross)
    operands = (near[0], far[0], near[0], far[0])
    total, got = yield from reduce_chips(z, 0, lambda li: (li & 1) == 1, operands)
    cut = z.share_rows // 2
    share = jnp.concatenate([total[cut:], got[cut:]], axis=0)
    share = yield from sent(z, share.astype(BF), lambda dp, li: (dp, 0) if li == 1 else None)
    return share.astype(F32), jnp.concatenate([total[:cut], got[:cut]], axis=0)


def sum_of_own_layer(z, stacked, place):
    bit = 0
    while (1 << bit) < z.cycle:
        mine = (place >> bit) & 1
        pairs = stacked.reshape((stacked.shape[0] // 2, 2) + stacked.shape[1:])
        own = lax.dynamic_index_in_dim(pairs, mine, 1, keepdims=False)
        other = lax.dynamic_index_in_dim(pairs, 1 - mine, 1, keepdims=False)
        got = yield from sent(z, other, lambda dp, li: (dp, li ^ (1 << bit)))
        stacked = own + got
        bit += 1
    return stacked[0]


class Chain:
    def __init__(self, steps):
        self.steps, self.result = steps, None
        self.leaving, self.arriving = next(steps)

    def go_on(self, arrived):
        try:
            self.leaving, self.arriving = self.steps.send(arrived)
        except StopIteration as end:
            self.leaving, self.arriving, self.result = [], [], end.value


def advance(chains, *tokens):
    chains = [chain for chain in chains if chain.arriving]
    if not chains:
        return []
    sizes = [len(chain.arriving) for chain in chains]
    arrived = list(lax.optimization_barrier((*sum((chain.arriving for chain in chains), []), *tokens)))
    marks = [arrived[0]]
    for chain, size in zip(chains, sizes):
        chain.go_on(arrived[:size])
        arrived = arrived[size:]
    return marks


def reduce_whole(z, stay, cross):
    rows = jnp.concatenate([stay, cross], axis=0)
    rows = rows.reshape(z.blocks, 2 * rows.shape[1], LANES)
    at = rows.shape[1] - z.share_first
    mix = rows[:, at + z.x_rows :].reshape(z.blocks, z.m_fold, z.m_rows, LANES)
    mix = mix.transpose(0, 2, 1, 3).reshape(z.mixed_rows, z.res)
    bias = rows[:, at + z.x_rows - 1, : z.m_rows].reshape(z.mixed_rows)
    wide = rows[:, : at + z.x_rows].transpose(0, 2, 1).reshape(z.gate, at + z.x_rows)
    out = []
    for part in (wide, mix, bias):
        part = lax.psum(part.astype(F32), "layer").astype(BF)
        out.append(lax.psum_scatter(part, "dp", scatter_dimension=0, tiled=True).astype(F32))
    return tuple(out)


def sum_of_all(z, values):
    moves = [(0, 1)]
    moves += [(1 << b, 0) for b in range(1, z.data.bit_length() - 1)] + [(1, 0)]
    moves += [(0, 1 << b) for b in range(1, z.cycle.bit_length() - 1)]
    for a, b in moves:
        values = values + (yield from sent(z, values, lambda dp, li: (dp ^ a, li ^ b)))
    return values


def per_device(*args):
    (
        audio_in,
        mel_spec,
        lengths,
        z_cotangent,
        det_cotangent,
        lu_weight,
        start_weight,
        start_bias,
        in_weight,
        cond_weight,
        gate_bias,
        mix_weight,
        mix_bias,
        end_weight,
        end_bias,
    ) = args
    cycle, data = lax.axis_size("layer"), lax.axis_size("dp")
    z = Sizes(args, cycle, data)
    place, group_place = lax.axis_index("layer"), lax.axis_index("dp")
    scalars = jnp.stack([place, group_place, place // z.copies]).astype(jnp.int32)
    in_w, mix = in_weight[0], mix_weight[0]
    start_rows = jnp.concatenate([start_weight.T, start_bias[None], jnp.zeros((7 - z.half, z.res), F32)], axis=0)
    det_row = det_cotangent[None, :]
    ends = jnp.concatenate([end_weight, end_weight, end_weight, jnp.zeros((LANES - z.group, z.mixed_rows), BF)], axis=0)

    def prepared():
        pack, start_x = prepare_weights(z, in_w, cond_weight, gate_bias, mix, mix_bias, start_rows, end_weight)(
            scalars, in_w, cond_weight[0], gate_bias, mix, mix_bias, start_rows, end_weight
        )
        x, mixed, masks, turned, matrix = prepare_frames(z)(scalars, lengths, audio_in, mel_spec, lu_weight)
        return pack, x, start_x, mixed, masks, turned, matrix

    (_, x, start_x, mixed, masks, turned, matrix), packs, early, far_late = near_weights(
        z, in_w, group_place, prepared
    )

    packs, (x, masks, turned) = in_hbm(packs), in_hbm((x, masks, turned))
    *saved, totals = forward_group(z, len(early), len(packs))(scalars, *early, *packs, x, masks, start_x)
    saved = [in_hbm(saved[4 * layer : 4 * layer + 4]) for layer in range(cycle - 1)]
    late = late_weights(z, early, far_late, totals)

    own = None
    if z.copies > 1:
        own = ((place % z.copies) == 0).astype(F32)
    mine = lambda v: v if own is None else (v * own.astype(v.dtype))
    blocks, after = {}, []
    for high in range(cycle - 1, 0, -2):
        low = high - 1
        if z.direct and not low:
            while own_outer.result is None:
                advance([own_outer])
            advance([pair], own_outer.result)
            after = [*pair.leaving]
        at_high = late if high == cycle - 1 else early
        at_low = late if low == 0 else early
        kernel = gradient_group(z, high, len(after), len(at_high), len(at_low), len(packs))
        ins = [*after, *at_high, *at_low, *packs, x, masks, ends, saved[low][3]]
        if high == cycle - 1:
            ins += [totals, z_cotangent, det_row, mixed, end_bias[:, None], lu_weight]
            ins += [saved[other][0] for other in range(cycle - 2)]
        else:
            ins += in_hbm([dres, h, dx]) + saved[high][:3]
        ins += saved[low][:3]
        if low:
            ins += [saved[low - 1][3], turned]
        else:
            ins += [turned, start_x, base, matrix, audio_in, lu_weight, det_row]
        stay, cross, *outs = kernel(scalars, *ins)
        blocks[high] = (mine(stay), mine(cross))
        if low:
            h, dx, *outs = outs
        else:
            tail, mel_grad, audio_grad = outs
        if high == cycle - 1:
            outer, a_part, latent, logdet, dres, base = outs
            dsum_rows = jnp.broadcast_to(a_part[:, z.ones : z.ones + 1], (cycle, z.group, z.res))
            own_outer = Chain(sum_of_own_layer(z, mine(jnp.concatenate([outer, dsum_rows], axis=1)), place))
            if z.direct:
                pair = Chain(reduce_last_two(z, *blocks[high]))

    if z.direct:
        token = advance([pair], tail)
        tail = tie(tail, *token)
        blocks[1] = [tie(block, *token) for block in blocks[1]]
    else:
        token = []
        while own_outer.result is None:
            token = advance([own_outer], *token)
    end_part = finish(z)(scalars, own_outer.result, mix, mix_bias, start_rows, mine(a_part))
    small = Chain(sum_of_all(z, jnp.concatenate([end_part, mine(tail)], axis=0)))
    active = [small]
    if z.direct:
        both = Chain(reduce_first_two(z, *blocks[1]))
        active += [both, pair]
    while any(chain.arriving for chain in active):
        token = advance(active, *token)
    whole_sum = small.result
    end_weight_grad = jnp.concatenate([whole_sum[0:8], whole_sum[8:16, : z.skip]], axis=1)
    lu_grad = whole_sum[24:32, : z.group]
    end_bias_grad = whole_sum[24, LANES : LANES + z.group]
    start_weight_grad = whole_sum[16 : 16 + z.half].T
    start_bias_grad = whole_sum[16 + z.half]

    if z.direct:
        first_share, share = both.result
        share = jnp.where(place >= 2, pair.result, share)
        short = jnp.where(place == 0, first_share, share[z.taps :])
        conds = short[: z.x_rows].T
        mix_grad = short[z.x_rows :].reshape(z.m_fold, z.m_rows, LANES)
        mix_grad = jnp.concatenate([mix_grad[j] for j in range(z.m_fold)], axis=1)
        mix_bias_grad = short[z.x_rows - 1, : z.m_rows]
        in_grad = share[: z.taps].T
    else:
        wide = mix_grad = mix_bias_grad = None
        for layer in range(cycle):
            high = layer + (layer + 1) % 2
            rows = z.share_rows // 2
            stay, cross = blocks[high]
            if high > 1:
                stay, cross = stay[high - layer], cross[high - layer]
            elif layer:
                stay, cross = stay[:, :rows], cross[:, :rows]
            else:
                stay, cross = stay[:, rows:], cross[:, rows:]
            new = reduce_whole(z, stay, cross)
            if not layer:
                wide, mix_grad, mix_bias_grad = (jnp.pad(new[0], ((0, 0), (z.taps, 0))), *new[1:])
                continue
            wide, mix_grad, mix_bias_grad = jax.tree.map(
                lambda now, old: jnp.where(place == layer, now, old), new, (wide, mix_grad, mix_bias_grad)
            )
        in_grad, conds = wide[:, : z.taps], wide[:, z.taps :]
    rows = conds[:, z.first : z.first + 3 * z.tap_rows].reshape(-1, 3, z.tap_rows)
    half = z.half
    rows = jnp.concatenate([rows[:, :, :half] + rows[:, :, half : 2 * half], rows[:, :, 3 * half : 3 * half + 1]], 2)
    first_in_grad = jnp.einsum("rkj,jc->rkc", rows, start_rows[: half + 1], precision=highest).reshape(-1, z.taps)
    in_grad = jnp.where(place == 0, first_in_grad, in_grad)

    def own_columns(rows):
        if z.copies == 1:
            return rows
        width = z.frames // z.copies
        return lax.dynamic_slice_in_dim(rows, (place % z.copies) * width, width, 1)

    return (
        own_columns(latent),
        own_columns(logdet)[0],
        own_columns(audio_grad),
        own_columns(mel_grad),
        lu_grad,
        start_weight_grad,
        start_bias_grad,
        in_grad[None],
        conds[None, :, : z.mel],
        conds[None, :, z.ones],
        mix_grad[None],
        mix_bias_grad[None],
        end_weight_grad,
        end_bias_grad,
    )


def solution(mesh):
    in_specs = (
        P(None, "dp"),
        P(None, "dp"),
        P("dp", None),
        P(None, "dp"),
        P("dp"),
        P(),
        P(),
        P(),
        P("layer", None, None),
        P("layer", None, None),
        P("layer", None),
        P("layer", None, None),
        P("layer", None),
        P(),
        P(),
    )
    out_specs = (
        P(None, ("dp", "layer")),
        P(("dp", "layer")),
        P(None, ("dp", "layer")),
        P(None, ("dp", "layer")),
        P(),
        P(),
        P(),
        P("layer", "dp", None),
        P("layer", "dp", None),
        P("layer", "dp"),
        P("layer", "dp", None),
        P("layer", "dp"),
        P(),
        P(),
    )
    return jax.shard_map(
        per_device, mesh=mesh, in_specs=in_specs, out_specs=out_specs, check_vma=False
    )
```

```python
import functools

import jax
import jax.numpy as jnp
from jax import lax
from jax.experimental import pallas as pl
from jax.experimental.pallas import tpu as pltpu
from jax.sharding import PartitionSpec as P

BF = jnp.bfloat16
F32 = jnp.float32
LANES = 128
MISC = 48
MIB = 1 << 20
highest = lax.Precision.HIGHEST
VMEM = pltpu.VMEM
ANY = pl.ANY


def mm(first, second, first_dim=1, second_dim=0):
    return lax.dot_general(
        first, second, (((first_dim,), (second_dim,)), ((), ())), preferred_element_type=F32
    )


def split_high_low(values):
    high = values.astype(BF)
    return high, (values - high.astype(F32)).astype(BF)


def kept(rows, cols, dtype=BF):
    return pltpu.HBM((rows, cols), dtype)


def whole(space=VMEM):
    return pl.BlockSpec(memory_space=space)


def call(body, name, out_shape, scratch, grid=None, in_specs=None, out_specs=None, flops=0, nbytes=0, vmem=24):
    return pl.pallas_call(
        body,
        name=name,
        out_shape=out_shape,
        grid_spec=pltpu.PrefetchScalarGridSpec(
            num_scalar_prefetch=1,
            grid=grid or (1,),
            in_specs=in_specs,
            out_specs=out_specs,
            scratch_shapes=scratch,
        ),
        compiler_params=pltpu.CompilerParams(vmem_limit_bytes=vmem * MIB),
        cost_estimate=pl.CostEstimate(
            flops=int(flops), bytes_accessed=int(nbytes), transcendentals=0
        ),
    )


class Sizes:
    def __init__(self, args, cycle, data):
        (audio, mel, lengths, _, _, _, start_weight, _, in_weight, _, _, mix_weight) = args[:12]
        self.cycle, self.data = cycle, data
        self.micro, self.utts = lengths.shape
        self.copies = cycle // self.micro
        assert self.copies * self.micro == cycle
        self.frames = audio.shape[1] // self.micro
        self.group = audio.shape[0]
        self.half = self.group // 2
        self.mel = mel.shape[0]
        self.res = start_weight.shape[0]
        self.gate = in_weight.shape[1]
        self.taps = in_weight.shape[2]
        self.mixed_rows = mix_weight.shape[1]
        self.skip = self.mixed_rows - self.res
        self.ones = self.mel
        self.tap_rows = 3 * self.half + 2
        self.first = self.mel + 2
        self.x_rows = -(-(self.first + 3 * self.tap_rows) // LANES) * LANES
        self.all_rows = self.taps + self.x_rows
        self.pack_misc = self.res
        self.pack_cond = self.res + MISC
        self.me_rows = self.res + LANES
        self.cond_blocks = self.res // self.x_rows
        self.cond_rows = self.gate // self.cond_blocks
        self.pack_rows = self.pack_cond + self.cond_rows
        self.blocks = self.gate // LANES
        self.m_rows = self.mixed_rows // self.blocks
        self.m_fold = self.res // LANES
        self.m_pack = self.m_rows * self.m_fold
        self.share_first = self.x_rows + self.m_pack
        self.share_rows = self.taps + self.share_first
        self.direct = cycle == 4 and data == self.blocks
        self.bits = data.bit_length() - 1

    def tap(self, number):
        return self.first + number * self.tap_rows


def prepare_weights(z, in_w, cond, gate_bias, mix, mix_bias, start, end_w):
    def body(s_ref, in_ref, cond_ref, gb_ref, mix_ref, mb_ref, start_ref, end_ref, pack_ref, sx_ref, acc, in_v, sem):
        start_high, start_low = split_high_low(start_ref[...])
        start_pair = jnp.concatenate([start_high.astype(F32), start_low.astype(F32)], axis=0).astype(BF)
        in_copy = pltpu.make_async_copy(in_ref, in_v, sem)

        @pl.when(s_ref[0] == 0)
        def _():
            in_copy.start()

        col = lax.broadcasted_iota(jnp.int32, (8, z.x_rows), 1)

        row16 = lax.broadcasted_iota(jnp.int32, (16, z.x_rows), 0)
        col16 = lax.broadcasted_iota(jnp.int32, (16, z.x_rows), 1)

        def spread(tap):
            base, h = z.tap(tap), z.half
            spot = jnp.where(col16 < base + 3 * h, lax.rem(col16 - base + 3 * h, h), h)
            inside = (col16 >= base) & (col16 < base + z.tap_rows)
            hit = (inside & ((row16 & 7) == spot)).astype(F32).astype(BF)
            return mm(start_pair, hit, 0, 0)

        def is_low(tap):
            base = z.tap(tap)
            return ((col >= base + 2 * z.half) & (col < base + 3 * z.half)) | (col == base + 3 * z.half + 1)

        def choose(values, low_cols):
            high = values.astype(BF).astype(F32)
            return jnp.where(low_cols, values - high, high).astype(BF)

        eye = (
            lax.broadcasted_iota(jnp.int32, (z.mel, z.x_rows), 0)
            == lax.broadcasted_iota(jnp.int32, (z.mel, z.x_rows), 1)
        ).astype(F32).astype(BF)
        bias = gb_ref[...]
        bias_high = bias.astype(BF).astype(F32)
        bias_rows = jnp.concatenate([bias_high, bias - bias_high, jnp.zeros((14, z.gate), F32)], axis=0)
        pick = (((row16 == 0) & (col16 == z.ones)) | ((row16 == 1) & (col16 == z.ones + 1))).astype(F32)
        acc[...] = mm(cond_ref[...], eye) + mm(bias_rows.astype(BF), pick.astype(BF), 0, 0)
        middle = spread(1)
        end_res = end_ref[:, 0 : z.res]
        high, low = split_high_low(middle)
        ends_start = mm(end_res, high) + mm(end_res, low)
        sx_ref[0 : z.res, :] = choose(middle, is_low(1)[0:1, :])
        sx_ref[z.res :, :] = jnp.concatenate([choose(ends_start, is_low(1)).astype(F32), jnp.zeros((8, z.x_rows), F32)], axis=0).astype(BF)
        pack_ref[0 : z.res, :] = mix_ref[0 : z.res, :]
        ends = mm(end_ref[...], mix_ref[...])
        ends_high = ends.astype(BF).astype(F32)
        bias_end = jnp.sum(end_ref[...].astype(F32) * mb_ref[...], axis=1, keepdims=True)
        bias_end = jnp.broadcast_to(bias_end, (z.group, z.res))
        bias_end_high = bias_end.astype(BF).astype(F32)
        own = mb_ref[:, 0 : z.res]
        own_high = own.astype(BF).astype(F32)
        pack_ref[z.pack_misc : z.pack_misc + 16, :] = jnp.concatenate([ends_high, ends - ends_high], axis=0).astype(BF)
        pack_ref[z.pack_misc + 16 : z.pack_misc + 32, :] = jnp.concatenate(
            [bias_end_high, bias_end - bias_end_high], axis=0
        ).astype(BF)
        pack_ref[z.pack_misc + 32 : z.pack_misc + 48, :] = jnp.concatenate(
            [own_high, own - own_high, jnp.zeros((14, z.res), F32)], axis=0
        ).astype(BF)

        @pl.when(s_ref[0] == 0)
        def _():
            in_copy.wait()
            for tap in range(3):
                high, low = split_high_low(spread(tap))
                block = in_v[:, tap * z.res : (tap + 1) * z.res]
                acc[...] += mm(block, high) + mm(block, low)

        low_cols = (is_low(0) | is_low(1) | is_low(2))[0:1, :]
        cond_x = choose(acc[...], low_cols)
        for j in range(z.cond_blocks):
            pack_ref[z.pack_cond :, j * z.x_rows : (j + 1) * z.x_rows] = cond_x[
                j * z.cond_rows : (j + 1) * z.cond_rows
            ]

    return call(
        body,
        "prepare_weights",
        (
            kept(z.pack_rows, z.res),
            jax.ShapeDtypeStruct((z.res + 16, z.x_rows), BF),
        ),
        [pltpu.VMEM((z.gate, z.x_rows), F32), pltpu.VMEM((z.gate, z.taps), BF), pltpu.SemaphoreType.DMA],
        in_specs=[whole(ANY)] + [whole()] * 6,
        out_specs=(whole(), whole()),
        flops=2 * z.gate * z.taps * z.x_rows,
        nbytes=6 * MIB,
    )


def prepare_frames(z):
    def body(s_ref, len_ref, audio_ref, mel_ref, lu_ref, x_ref, mixed_ref, mask_ref, turned_ref, matrix_ref, tall):
        lu = lu_ref[...]
        r = lax.broadcasted_iota(jnp.int32, lu.shape, 0)
        c = lax.broadcasted_iota(jnp.int32, lu.shape, 1)
        lower = jnp.where(r > c, lu, 0.0) + jnp.where(r == c, 1.0, 0.0)
        upper = jnp.where(r < c, lu, 0.0) + jnp.where(r == c, jnp.exp(lu), 0.0)
        matrix = lower[:, 0:1] * upper[0:1, :]
        for k in range(1, z.group):
            matrix = matrix + lower[:, k : k + 1] * upper[k : k + 1, :]
        matrix_ref[...] = matrix
        mixed = matrix[:, 0:1] * audio_ref[0:1, :]
        for k in range(1, z.group):
            mixed = mixed + matrix[:, k : k + 1] * audio_ref[k : k + 1, :]
        mixed_ref[...] = mixed
        place = lax.broadcasted_iota(jnp.int32, (16, z.frames), 1)
        begin = jnp.int32(0)
        left = jnp.zeros((16, z.frames), jnp.int32)
        right = jnp.zeros((16, z.frames), jnp.int32)
        for u in range(z.utts):
            size = len_ref[s_ref[2], u]
            inside = (place >= begin) & (place < begin + size)
            left = jnp.where(inside, place - begin, left)
            right = jnp.where(inside, begin + size - 1 - place, right)
            begin = begin + size
        for l in range(z.cycle):
            mask_ref[l, 0:16, :] = (left >= 2**l).astype(F32).astype(BF)
            mask_ref[l, 16:32, :] = (right >= 2**l).astype(F32).astype(BF)
        tall[...] = jnp.zeros_like(tall)
        for l in range(z.cycle):
            tall[2 * l : 2 * l + 1, :] = (left >= 2**l).astype(F32)[0:1]
            tall[2 * l + 1 : 2 * l + 2, :] = (right >= 2**l).astype(F32)[0:1]
        turned_ref[...] = tall[...].T
        high = mixed.astype(BF).astype(F32)
        low = (mixed - high).astype(BF).astype(F32)
        tall[...] = jnp.zeros_like(tall)
        tall[0 : z.mel, :] = mel_ref[...].astype(F32)
        tall[z.ones : z.ones + 2, :] = jnp.ones((2, z.frames), F32)
        masks = ((left >= 1).astype(F32)[0:8], jnp.ones((8, z.frames), F32), (right >= 1).astype(F32)[0:8])
        for tap in range(3):
            shift = (1, 0, z.frames - 1)[tap]
            moved_high = (pltpu.roll(high, shift, axis=1) if shift else high) * masks[tap]
            moved_low = (pltpu.roll(low, shift, axis=1) if shift else low) * masks[tap]
            base = z.tap(tap)
            h = z.half
            tall[base : base + h, :] = moved_high[0:h]
            tall[base + h : base + 2 * h, :] = moved_low[0:h]
            tall[base + 2 * h : base + 3 * h, :] = moved_high[0:h]
            tall[base + 3 * h : base + 3 * h + 2, :] = masks[tap][0:2]
        x_ref[...] = tall[...].astype(BF)

    def column(rows):
        return pl.BlockSpec((rows, z.frames), lambda i, s: (0, s[2]))

    return call(
        body,
        "prepare_frames",
        (
            kept(z.x_rows, z.frames),
            jax.ShapeDtypeStruct((z.group, z.frames), F32),
            pltpu.HBM((z.cycle, 32, z.frames), BF),
            kept(z.frames, z.x_rows, F32),
            jax.ShapeDtypeStruct((z.group, z.group), F32),
        ),
        [pltpu.VMEM((z.x_rows, z.frames), F32)],
        in_specs=[whole(pltpu.SMEM), column(z.group), column(z.mel), whole()],
        out_specs=(whole(),) * 5,
        flops=1e6,
        nbytes=2 * MIB,
    )


def taps_copies(z, s_ref, sources, layer, target, sem):
    if len(sources) == 1:
        return [pltpu.make_async_copy(sources[0].at[layer], target, sem)], None
    copy = pltpu.make_async_copy
    if len(sources) == 4:
        return [[copy(source, target, sem)] for source in sources], s_ref[0] ^ layer
    own, near, far, beside, cross, cross_beside = sources
    rows = z.gate // 2
    x = s_ref[1] & 1
    mine = target.at[pl.ds(pl.multiple_of(x * rows, rows), rows)]
    other = target.at[pl.ds(pl.multiple_of((1 - x) * rows, rows), rows)]
    slots = [
        [copy(own, target, sem)],
        [copy(near, target, sem)],
        [copy(far, mine, sem), copy(beside, other, sem)],
        [copy(cross, mine, sem), copy(cross_beside, other, sem)],
    ]
    return slots, s_ref[0] ^ layer


def pack_copies(z, s_ref, packs, layer, me, wide, column, sems):
    def of(ref):
        conds = [
            pltpu.make_async_copy(
                ref.at[pl.ds(z.pack_cond, z.cond_rows), pl.ds(j * z.x_rows, z.x_rows)],
                wide.at[pl.ds(j * z.cond_rows, z.cond_rows), pl.ds(column, z.x_rows)],
                sems.at[0],
            )
            for j in range(z.cond_blocks)
        ]
        return conds + [
            pltpu.make_async_copy(ref.at[pl.ds(0, z.pack_cond)], me.at[pl.ds(0, z.pack_cond)], sems.at[1])
        ]

    if len(packs) == 1:
        return of(packs[0].at[layer]), None
    return [of(ref) for ref in packs], s_ref[0] ^ layer


def each(copies, action):
    chosen, slot = copies
    if slot is None:
        for copy in chosen:
            getattr(copy, action)()
        return
    for number, group in enumerate(chosen):

        @pl.when(slot == number)
        def _():
            for copy in group:
                getattr(copy, action)()


def fill_taps(z, taps, mask, layer):
    dilation = 2**layer
    rows = 128

    def one(i, _):
        begin = pl.multiple_of(i * rows, rows)
        block = taps[pl.ds(z.res + begin, rows), :]
        before = pltpu.roll(block, dilation, axis=1).reshape(rows // 16, 16, z.frames)
        after = pltpu.roll(block, z.frames - dilation, axis=1).reshape(rows // 16, 16, z.frames)
        taps[pl.ds(begin, rows), :] = (before * mask[0:16, :][None]).reshape(rows, z.frames)
        taps[pl.ds(2 * z.res + begin, rows), :] = (after * mask[16:32, :][None]).reshape(rows, z.frames)
        return 0

    lax.fori_loop(0, z.res // rows, one, 0)


class Copies:
    def __init__(self, sems):
        self.sems, self.used = sems, 0

    def start(self, source, target):
        copy = pltpu.make_async_copy(source, target, self.sems.at[self.used])
        self.used += 1
        copy.start()
        return copy

    def weights(self, z, s_ref, sources, packs, layer, wide, me, column):
        pack = pack_copies(z, s_ref, packs, layer, me, wide, column, self.sems.at[pl.ds(self.used, 2)])
        self.used += 2
        each(pack, "start")
        if not layer:
            return pack, None
        taps = taps_copies(z, s_ref, sources, layer, wide.at[:, pl.ds(0, z.taps)], self.sems.at[self.used])
        self.used += 1
        each(taps, "start")
        return pack, taps


def gate_parts(first, second):
    tanh = jnp.tanh(first)
    sig = 0.5 * jnp.tanh(0.5 * second) + 0.5
    gated = tanh * sig
    return gated.astype(BF), (sig - gated * tanh).astype(BF), (gated - gated * sig).astype(BF)


def bias_column(z, me):
    row = lax.broadcasted_iota(jnp.int32, (16, LANES), 0)
    pick = (row < 2).astype(F32).astype(BF)
    return mm(me[z.pack_misc + 32 : z.pack_misc + 48, :], pick, 0, 0)[:, 0:1]


def bias_end(z, me):
    rows = me[z.pack_misc + 16 : z.pack_misc + 32, :].astype(F32)
    return (rows[0 : z.group] + rows[z.group : 2 * z.group])[:, 0:1]


def forward_parts(z, layer, wide, taps, me, pre, add_end, start_of, save, gated_v, fa_v, fb_v, out_v, total):
    width = pre.shape[2]
    parts = z.frames // width
    mix_rows = 0 if layer == z.cycle - 1 else z.res
    add_stream = bias_column(z, me) if mix_rows else None

    def product(part):
        pre[part % 2, :, :] = mm(wide[...], taps[:, part * width : (part + 1) * width])

    product(0)
    for part in range(parts):
        if part + 1 < parts:
            product(part + 1)
        here = slice(part * width, (part + 1) * width)
        gated, fa, fb = gate_parts(pre[part % 2, 0 : z.res, :], pre[part % 2, z.res :, :])
        gated_v[:, here] = gated
        fa_v[here, :] = fa.T
        fb_v[here, :] = fb.T
        branch = mm(me[z.res - mix_rows : z.res + 16, :], gated)
        ends = branch[mix_rows : mix_rows + z.group] + branch[mix_rows + z.group :] + add_end
        if start_of is None:
            total[:, here] = total[:, here] + ends
        else:
            start = start_of(here)
            total[:, here] = ends + start[z.res : z.res + z.group]
        if mix_rows:
            stream = taps[z.res : 2 * z.res, here].astype(F32) if start_of is None else start[0 : z.res]
            if start_of is not None:
                stream = stream.astype(BF).astype(F32)
            out_v[:, here] = (stream + branch[0 : z.res] + add_stream).astype(BF)
        save(part)


def forward_group(z, n_sources, n_packs):
    width = 256
    parts = z.frames // width
    count = z.cycle - 1

    def body(s_ref, *refs):
        refs = list(refs)
        take = lambda n: [refs.pop(0) for _ in range(n)]
        sources, packs = take(n_sources), take(n_packs)
        (x_ref, mask_ref, sx_ref) = take(3)
        kept_refs = [take(4) for _ in range(count)]
        (total,) = take(1)
        (wides, first_wide, all_taps, x_v, mes, pre, gated_vs, fa_vs, fb_vs, masks, sems) = take(11)
        copies = Copies(sems)
        pending = {0: copies.weights(z, s_ref, sources, packs, 0, first_wide, mes.at[0], 0)}
        x_in = copies.start(x_ref, x_v)
        mask_in = copies.start(mask_ref, masks)
        x_taps = [copies.start(x_ref, all_taps.at[k, pl.ds(z.taps, z.x_rows)]) for k in range(2)]

        def bring(layer):
            k = layer % 2
            pending[layer] = copies.weights(z, s_ref, sources, packs, layer, wides.at[k], mes.at[k], z.taps)

        if count > 1:
            bring(1)
        x_in.wait()
        saves = {}
        for layer in range(count):
            k = layer % 2
            pack, taps_in = pending[layer]
            if layer and layer + 1 < count:
                bring(layer + 1)
            me = mes.at[k]
            taps = all_taps.at[k] if layer else x_v
            wide = wides.at[k] if layer else first_wide
            if layer == 1:
                mask_in.wait()
                for copy in x_taps:
                    copy.wait()
            if layer:
                fill_taps(z, taps, masks.at[layer], layer)
            each(pack, "wait")
            if layer:
                each(taps_in, "wait")
            for done in (layer - 1, layer - 2):
                for copy in saves.pop(done, []):
                    copy.wait()
            gated_v, fa_v, fb_v = gated_vs.at[k], fa_vs.at[k], fb_vs.at[k]
            out_v = all_taps.at[1 - k, pl.ds(z.res, z.res)]
            gated_ref, fa_ref, fb_ref, out_ref = kept_refs[layer]
            mine = saves[layer] = []

            def save(part):
                at = pl.ds(part * width, width)
                mine.append(copies.start(gated_v.at[:, at], gated_ref.at[:, at]))
                mine.append(copies.start(fa_v.at[at], fa_ref.at[at]))
                mine.append(copies.start(fb_v.at[at], fb_ref.at[at]))
                mine.append(copies.start(out_v.at[:, at], out_ref.at[:, at]))

            start_of = None if layer else (lambda here: mm(sx_ref[...], x_v[:, here]))
            forward_parts(
                z, layer, wide, taps, me, pre, bias_end(z, me), start_of, save, gated_v, fa_v, fb_v, out_v, total
            )
        for group in saves.values():
            for copy in group:
                copy.wait()
        if count == 1:
            mask_in.wait()
            for copy in x_taps:
                copy.wait()

    outs, out_specs = [], []
    for _ in range(count):
        outs += [kept(z.res, z.frames), kept(z.frames, z.res), kept(z.frames, z.res), kept(z.res, z.frames)]
        out_specs += [whole(ANY)] * 4
    outs.append(jax.ShapeDtypeStruct((z.group, z.frames), F32))
    out_specs.append(whole())
    return call(
        body,
        "forward_group",
        tuple(outs),
        [
            pltpu.VMEM((2, z.gate, z.all_rows), BF),
            pltpu.VMEM((z.gate, z.x_rows), BF),
            pltpu.VMEM((2, z.all_rows, z.frames), BF),
            pltpu.VMEM((z.x_rows, z.frames), BF),
            pltpu.VMEM((2, z.me_rows, z.res), BF),
            pltpu.VMEM((2, z.gate, width), F32),
            pltpu.VMEM((2, z.res, z.frames), BF),
            pltpu.VMEM((2, z.frames, z.res), BF),
            pltpu.VMEM((2, z.frames, z.res), BF),
            pltpu.VMEM((z.cycle, 32, z.frames), BF),
            pltpu.SemaphoreType.DMA((8 + count * (4 * parts + 3),)),
        ],
        in_specs=[whole(ANY)] * (n_sources + n_packs + 2) + [whole()],
        out_specs=tuple(out_specs),
        flops=8 * count * z.frames * z.gate * z.taps,
        nbytes=40 * MIB,
        vmem=50,
    )


def gradient_group(z, high, n_after, n_high, n_low, n_packs):
    low = high - 1
    last, first = high == z.cycle - 1, low == 0
    width = 256
    shares = z.blocks // 2
    half_rows = z.share_rows // 2
    extra = z.share_first // 2 if first else 0

    def body(s_ref, *refs):
        refs = list(refs)
        take = lambda n: [refs.pop(0) for _ in range(n)]
        take(n_after)
        sources = {high: take(n_high), low: take(n_low)}
        packs = take(n_packs)
        (x_ref, mask_ref, end_ref, stream_high) = take(4)
        if last:
            (res_ref, zcot_ref, cot_det_ref, mixed_ref, endb_ref, lu_ref) = take(6)
            other_gated = take(z.cycle - 2)
        else:
            (dres_in, h_in, dx_in) = take(3)
            saved_high = take(3)
        saved_low = take(3)
        if first:
            (turned_in, sx_ref, base_ref, matrix_ref, audio_ref, lu_ref, det_ref) = take(7)
        else:
            (stream_low, turned_in) = take(2)
        (stay_ref, cross_ref) = take(2)
        if first:
            (tail_ref, mel_ref, agrad_ref) = take(3)
        else:
            (h_out, dx_out) = take(2)
        if last:
            (p_ref, a_ref, latent_ref, logdet_ref, dres_out, base_out) = take(6)
        (wides, mes, all_taps, gated_vs, fa_vs, fb_vs, dpre, grads, hs, dx_ref, turned, dres_ref, masks, sems) = take(14)
        if last:
            (pre, total, spare) = take(3)
        if first:
            (low_wide, low_grads, in_v) = take(3)
        copies = Copies(sems)

        mask_in = copies.start(mask_ref, masks)
        high_in = [copies.start(stream_high, all_taps.at[0, pl.ds(z.res, z.res)])]
        if not last:
            gate_in = [copies.start(dres_in, dres_ref)]
        pack_high, taps_high = copies.weights(
            z, s_ref, sources[high], packs, high, wides.at[0], mes.at[0], z.taps
        )
        x_in = [copies.start(x_ref, all_taps.at[0, pl.ds(z.taps, z.x_rows)])]
        if not last:
            gate_in += [copies.start(h_in, hs.at[0, :, pl.ds(0, z.res)])]
            gate_in += [copies.start(a, b.at[0]) for a, b in zip(saved_high[1:], (fa_vs, fb_vs))]
            mix_in = [copies.start(saved_high[0], gated_vs.at[0]), copies.start(dx_in, dx_ref)]
        low_x = all_taps.at[0 if first else 1, pl.ds(z.taps, z.x_rows)]

        def fetch_low():
            turned_copy = copies.start(turned_in, turned)
            gate = [copies.start(a, b.at[1]) for a, b in zip(saved_low[1:], (fa_vs, fb_vs))]
            gate.append(copies.start(saved_low[0], gated_vs.at[1]))
            if first:
                pack, taps = copies.weights(z, s_ref, None, packs, 0, low_wide, mes.at[1], 0)
                taps = taps_copies(z, s_ref, sources[0], 0, in_v, sems.at[copies.used])
                copies.used += 1
                each(taps, "start")
                return turned_copy, gate, [], pack, taps
            fill = [
                copies.start(stream_low, all_taps.at[1, pl.ds(z.res, z.res)]),
                copies.start(x_ref, low_x),
            ]
            pack, taps = copies.weights(z, s_ref, sources[low], packs, low, wides.at[1], mes.at[1], z.taps)
            return turned_copy, gate, fill, pack, taps

        for k in range(2):
            mes[k, z.pack_cond :, :] = jnp.zeros((z.me_rows - z.pack_cond, z.res), BF)
        mask_in.wait()
        for copy in high_in:
            copy.wait()
        fill_taps(z, all_taps.at[0], masks.at[high], high)
        for copy in x_in:
            copy.wait()
        each(pack_high, "wait")
        if last:
            each(taps_high, "wait")
            mix_in = [copies.start(a, spare.at[i]) for i, a in enumerate(other_gated[:2])]
            turned_copy, gate_low, low_in, pack_low, taps_low = fetch_low()
            lu = lu_ref[...]
            r = lax.broadcasted_iota(jnp.int32, lu.shape, 0)
            c = lax.broadcasted_iota(jnp.int32, lu.shape, 1)
            trace = jnp.sum(jnp.where(r == c, lu, 0.0))
            total[...] = res_ref[...]
            forward_parts(
                z, high, wides.at[0], all_taps.at[0], mes.at[0], pre, bias_end(z, mes.at[0]) + endb_ref[...],
                None, lambda part: None, gated_vs.at[0], fa_vs.at[0], fb_vs.at[0], None, total,
            )
            h = z.half
            is_scale = lax.broadcasted_iota(jnp.int32, (z.group, z.frames), 0) < h
            turn = lambda rows: pltpu.roll(rows, h, axis=0)
            ends = total[...]
            growth = jnp.where(is_scale, jnp.exp(jnp.where(is_scale, ends, 0.0)), 0.0)
            mixed, zcot = mixed_ref[...], zcot_ref[...]
            grown = growth * turn(mixed)
            latent_ref[...] = jnp.where(is_scale, mixed, turn(grown) + ends)
            logdet_ref[...] = jnp.sum(jnp.where(is_scale, ends, 0.0), axis=0, keepdims=True) + trace
            dres = jnp.where(is_scale, turn(zcot) * grown + cot_det_ref[...], zcot)
            dres = jnp.concatenate([dres, dres, jnp.zeros((LANES - 16, z.frames), F32)], axis=0)
            dres_ref[...] = dres.T.astype(BF)
            base_out[...] = zcot * jnp.where(is_scale, 1.0, turn(growth))
            leaving = [copies.start(dres_ref, dres_out)]
        else:
            for copy in gate_in:
                copy.wait()
            turned_copy, gate_low, low_in, pack_low, taps_low = fetch_low()
            leaving = []
        for k in range(2):
            hs[k, :, z.res :] = dres_ref[...]

        two = lambda exact: jnp.concatenate(
            [exact.astype(BF).astype(F32), exact - exact.astype(BF).astype(F32)], axis=0
        ).astype(BF)
        dsum = jnp.sum(dres_ref[...].astype(F32), axis=0, keepdims=True)
        end_bias = mm(two(jnp.concatenate([dsum, jnp.zeros((7, LANES), F32)], axis=0)), end_ref[16:, :])
        end_bias = end_bias[0:8] + end_bias[8:16]

        def gate_and_mix(k, hd, has_h, grad_rows, at, ready):
            begin = 0 if has_h else z.res
            me = mes.at[k]
            for n in range(z.res // width):
                cols = slice(n * width, (n + 1) * width)
                dgated = mm(hd[:, begin:], me[begin:, cols])
                dpre[:, cols] = (dgated * fa_vs[k, :, cols].astype(F32)).astype(BF)
                dpre[:, z.res + n * width : z.res + (n + 1) * width] = (
                    dgated * fb_vs[k, :, cols].astype(F32)
                ).astype(BF)
            for copy in ready:
                copy.wait()
            both = mm(gated_vs[k], hd[:, begin:])
            outer = both[:, z.res - begin :].T[0 : z.group]
            mix_grad = mm(end_ref[0:16, :], two(outer), 0, 0)
            bias_grad = end_bias
            if has_h:
                mix_grad = mix_grad + jnp.concatenate([both[:, 0 : z.res].T, jnp.zeros((z.skip, z.res), F32)], axis=0)
                h_sum = jnp.sum(hd[:, 0 : z.res].astype(F32), axis=0, keepdims=True)
                h_sum = jnp.concatenate([h_sum, jnp.zeros((7, z.res), F32)], axis=0)
                bias_grad = bias_grad + jnp.concatenate([h_sum, jnp.zeros((8, z.skip), F32)], axis=1)
            mix_grad = mix_grad.astype(BF)
            for s in range(z.blocks):
                for j in range(z.m_fold):
                    top = at + j * z.m_rows
                    grad_rows[s, top : top + z.m_rows, :] = mix_grad[
                        s * z.m_rows : (s + 1) * z.m_rows, j * LANES : (j + 1) * LANES
                    ]
            return outer, bias_grad

        row = lax.broadcasted_iota(jnp.int32, (z.x_rows, LANES), 0)

        def with_bias(block, bias_grad, s):
            moved = pltpu.roll(bias_grad, (z.mixed_rows - s * z.m_rows) % z.mixed_rows, axis=1) if s else bias_grad
            return jnp.where(row == z.x_rows - 1, moved[0:1, 0:LANES], block).astype(BF)

        def taps_gradients(k, bias_grad):
            for n in range(z.gate // width):
                part = mm(all_taps[k], dpre[:, n * width : (n + 1) * width])
                for i in range(width // LANES):
                    s = n * (width // LANES) + i
                    lanes = slice(i * LANES, (i + 1) * LANES)
                    grads[s, 0 : z.taps, :] = part[0 : z.taps, lanes].astype(BF)
                    grads[s, z.taps : z.taps + z.x_rows, :] = with_bias(part[z.taps :, lanes], bias_grad, s)

        sent_sem = sems.at[copies.used]
        copies.used += 1

        def send(layer, grad_rows, rows, top):
            owner = max(layer, 1)
            away = (s_ref[0] ^ owner) & 1
            off_side = ((s_ref[0] ^ owner) >> 1) & 1
            for s in range(z.blocks):
                for half in range(2):
                    if z.direct:
                        v = s_ref[1] ^ s
                        place = (off_side ^ half) << (z.bits - 1)
                        for b in range(1, z.bits):
                            place = place | (((v >> b) & 1) << (z.bits - 1 - b))
                        to_stay = (v & 1) == away
                        role = away
                    else:
                        place, to_stay = jnp.int32((s % shares) * 2 + half), jnp.int32(s) < shares
                        role = jnp.int32(high - layer)
                    block = grad_rows.at[s, pl.ds(half * rows, rows)]
                    if first:
                        stay_at = stay_ref.at[place, pl.ds(top, rows)]
                        cross_at = cross_ref.at[place, pl.ds(top, rows)]
                    else:
                        stay_at = stay_ref.at[role, place]
                        cross_at = cross_ref.at[1 - role if z.direct else role, place]

                    @pl.when(to_stay)
                    def _():
                        pltpu.make_async_copy(block, stay_at, sent_sem).start()

                    @pl.when(jnp.logical_not(to_stay))
                    def _():
                        pltpu.make_async_copy(block, cross_at, sent_sem).start()

        def sent_wait(grad_rows, rows):
            target = stay_ref.at[0, pl.ds(0, rows)] if first else stay_ref.at[0, 0]
            for _ in range(2 * z.blocks):
                pltpu.make_async_copy(grad_rows.at[0, pl.ds(0, rows)], target, sent_sem).wait()

        def stream_gradient(layer, k, h_ref, new_h):
            d = 2**layer
            dx = mm(dpre[...], wides[k, :, z.taps :])
            dx_ref[...] = dx if layer == z.cycle - 1 else dx + dx_ref[...]
            keep_before = turned[:, 2 * layer : 2 * layer + 1]
            keep_after = turned[:, 2 * layer + 1 : 2 * layer + 2]
            for n in range(z.res // width):
                cols = slice(n * width, (n + 1) * width)
                side = [
                    mm(dpre[...], wides[k, :, i * z.res + n * width : i * z.res + (n + 1) * width]) for i in range(3)
                ]
                result = side[1] + pltpu.roll(side[0] * keep_before, z.frames - d, axis=0)
                result = result + pltpu.roll(side[2] * keep_after, d, axis=0)
                if h_ref is not None:
                    result = result + h_ref[:, cols].astype(F32)
                new_h[:, cols] = result.astype(BF)

        h_high = None if last else hs.at[0]
        outer, bias_grad = gate_and_mix(0, hs.at[0], not last, grads, z.taps + z.x_rows, [] if last else mix_in)
        if last:
            p_ref[high, :, :] = outer
            a_ref[...] = mm(all_taps[0, z.taps :, :], dres_ref[...]).T[0 : z.group]
            for i in range(z.cycle - 2):
                mix_in[i].wait()
                p_ref[i, :, :] = mm(spare[i % 2], dres_ref[...]).T[0 : z.group]
                if i + 2 < z.cycle - 2:
                    mix_in.append(copies.start(other_gated[i + 2], spare.at[i % 2]))
        taps_gradients(0, bias_grad)
        send(high, grads, half_rows, 0)
        turned_copy.wait()
        if not last:
            each(taps_high, "wait")
        stream_gradient(high, 0, h_high, hs.at[1])
        for copy in low_in:
            copy.wait()
        if not first:
            fill_taps(z, all_taps.at[1], masks.at[low], low)
        each(pack_low, "wait")
        for copy in gate_low:
            copy.wait()
        sent_wait(grads, half_rows)
        if not first:
            outer, bias_grad = gate_and_mix(1, hs.at[1], True, grads, z.taps + z.x_rows, [])
            if last:
                p_ref[low, :, :] = outer
            taps_gradients(1, bias_grad)
            send(low, grads, half_rows, 0)
            each(taps_low, "wait")
            stream_gradient(low, 1, hs.at[1], hs.at[0])
            leaving += [copies.start(hs.at[0, :, pl.ds(0, z.res)], h_out), copies.start(dx_ref, dx_out)]
            sent_wait(grads, half_rows)
        else:
            outer, bias_grad = gate_and_mix(1, hs.at[1], True, low_grads, z.x_rows, [])
            dcond = mm(low_x[...], dpre[...])
            for s in range(z.blocks):
                low_grads[s, 0 : z.x_rows, :] = with_bias(dcond[:, s * LANES : (s + 1) * LANES], bias_grad, s)
            send(0, low_grads, extra, half_rows)
            h = z.half
            g_first = hs.at[0, :, pl.ds(0, z.res)]
            g_first[...] = (hs[1, :, 0 : z.res].astype(F32) + mm(dres_ref[...], end_ref[16:, 0 : z.res])).astype(BF)
            dx = dx_ref[...] + mm(dpre[...], low_wide[...]) + mm(g_first[...], sx_ref[0 : z.res, :])
            dx = dx.T
            hx = mm(low_x[...], g_first[...])

            def folded(rows, tap):
                base = z.tap(tap)
                return [rows[base : base + h] + rows[base + h : base + 2 * h], rows[base + 3 * h : base + 3 * h + 1]]

            q = jnp.concatenate(
                folded(dcond, 0) + folded(dcond, 1) + folded(dcond, 2) + [jnp.zeros((16 - 3 * (h + 1), z.gate), F32)],
                axis=0,
            )
            each(taps_low, "wait")
            back = mm(two(q), in_v[...])
            start_rows = jnp.concatenate(folded(hx, 1), axis=0)
            for tap in range(3):
                top = tap * (h + 1)
                part = back[:, tap * z.res : (tap + 1) * z.res]
                start_rows = start_rows + part[top : top + h + 1] + part[16 + top : 16 + top + h + 1]
            tail_ref[...] = jnp.zeros_like(tail_ref)
            tail_ref[0 : h + 1, :] = start_rows
            mel_ref[...] = dx[0 : z.mel, :]
            keep_before = masks[0, 0:16, :].astype(F32)[0:h]
            keep_after = masks[0, 16:32, :].astype(F32)[0:h]
            tap_rows = []
            for tap in range(3):
                base = z.tap(tap)
                tap_rows.append(dx[base : base + h, :] + dx[base + 2 * h : base + 3 * h, :])
            zero = jnp.zeros((8 - h, z.frames), F32)
            pad = lambda v: jnp.concatenate([v, zero], axis=0)
            front = pad(tap_rows[1])
            front = front + pltpu.roll(pad(tap_rows[0] * keep_before), z.frames - 1, axis=1)
            front = front + pltpu.roll(pad(tap_rows[2] * keep_after), 1, axis=1)
            dmixed = front + base_ref[...]
            matrix = matrix_ref[...]
            r = lax.broadcasted_iota(jnp.int32, matrix.shape, 0)
            c = lax.broadcasted_iota(jnp.int32, matrix.shape, 1)
            flipped = matrix.T
            agrad = jnp.zeros((z.group, z.frames), F32)
            for k in range(z.group):
                agrad = agrad + flipped[:, k : k + 1] * dmixed[k : k + 1, :]
            agrad_ref[...] = agrad
            dmatrix = jnp.zeros((z.group, z.group), F32)
            for k in range(z.group):
                column = jnp.sum(dmixed * audio_ref[k : k + 1, :], axis=1, keepdims=True)
                dmatrix = dmatrix + jnp.where(c == k, column, 0.0)
            lu = lu_ref[...]
            lower = jnp.where(r > c, lu, 0.0) + jnp.where(r == c, 1.0, 0.0)
            grown = jnp.where(r == c, jnp.exp(lu), 0.0)
            upper = jnp.where(r < c, lu, 0.0) + grown
            upper_t = upper.T
            lower_t = lower.T
            dlower = jnp.zeros_like(lu)
            dupper = jnp.zeros_like(lu)
            for k in range(z.group):
                dlower = dlower + dmatrix[:, k : k + 1] * upper_t[k : k + 1, :]
                dupper = dupper + lower_t[:, k : k + 1] * dmatrix[k : k + 1, :]
            total_lu = jnp.where(r > c, dlower, 0.0) + jnp.where(r < c, dupper, 0.0) + dupper * grown
            tail_ref[8 : 8 + z.group, 0 : z.group] = total_lu + jnp.where(r == c, jnp.sum(det_ref[...]), 0.0)
            tail_ref[8:9, LANES : 2 * LANES] = dsum
            sent_wait(low_grads, extra)
        for copy in leaving:
            copy.wait()

    def column(rows):
        return pl.BlockSpec((rows, z.frames), lambda i, s: (0, s[2]))

    in_specs = [whole(ANY)] * (n_after + n_high + n_low + n_packs + 2) + [whole(), whole(ANY)]
    if last:
        in_specs += [whole(), column(z.group), column(1), whole(), whole(), whole()] + [whole(ANY)] * (z.cycle - 2)
    else:
        in_specs += [whole(ANY)] * 6
    in_specs += [whole(ANY)] * 3
    if first:
        in_specs += [whole(ANY), whole(), whole(), whole(), column(z.group), whole(), column(1)]
    else:
        in_specs += [whole(ANY)] * 2
    lead = () if first else (2,)
    outs = [pltpu.HBM((*lead, 2 * shares, half_rows + extra, LANES), BF)] * 2
    out_specs = [whole(ANY)] * 2
    if first:
        outs += [
            jax.ShapeDtypeStruct((16, z.res), F32),
            jax.ShapeDtypeStruct((z.mel, z.frames), F32),
            jax.ShapeDtypeStruct((z.group, z.frames), F32),
        ]
        out_specs += [whole()] * 3
    else:
        outs += [kept(z.frames, z.res), kept(z.frames, z.x_rows, F32)]
        out_specs += [whole(ANY)] * 2
    if last:
        outs += [
            jax.ShapeDtypeStruct((z.cycle, z.group, z.res), F32),
            jax.ShapeDtypeStruct((z.group, z.x_rows), F32),
            jax.ShapeDtypeStruct((z.group, z.frames), F32),
            jax.ShapeDtypeStruct((1, z.frames), F32),
            kept(z.frames, LANES),
            jax.ShapeDtypeStruct((z.group, z.frames), F32),
        ]
        out_specs += [whole()] * 4 + [whole(ANY), whole()]
    sets = 1 if first else 2
    scratch = [
        pltpu.VMEM((sets, z.gate, z.all_rows), BF),
        pltpu.VMEM((2, z.me_rows, z.res), BF),
        pltpu.VMEM((sets, z.all_rows, z.frames), BF),
        pltpu.VMEM((2, z.res, z.frames), BF),
        pltpu.VMEM((2, z.frames, z.res), BF),
        pltpu.VMEM((2, z.frames, z.res), BF),
        pltpu.VMEM((z.frames, z.gate), BF),
        pltpu.VMEM((z.blocks, z.share_rows, LANES), BF),
        pltpu.VMEM((2, z.frames, z.me_rows), BF),
        pltpu.VMEM((z.frames, z.x_rows), F32),
        pltpu.VMEM((z.frames, z.x_rows), F32),
        pltpu.VMEM((z.frames, LANES), BF),
        pltpu.VMEM((z.cycle, 32, z.frames), BF),
        pltpu.SemaphoreType.DMA((40,)),
    ]
    if last:
        scratch += [
            pltpu.VMEM((2, z.gate, width), F32),
            pltpu.VMEM((z.group, z.frames), F32),
            pltpu.VMEM((2, z.res, z.frames), BF),
        ]
    if first:
        scratch += [
            pltpu.VMEM((z.gate, z.x_rows), BF),
            pltpu.VMEM((z.blocks, z.share_first, LANES), BF),
            pltpu.VMEM((z.gate, z.taps), BF),
        ]
    return call(
        body,
        "gradient_first" if first else "gradient_last" if last else "gradient_group",
        tuple(outs),
        scratch,
        in_specs=in_specs,
        out_specs=tuple(out_specs),
        flops=(60 if last else 40) * z.frames * z.gate * z.taps,
        nbytes=20 * MIB,
        vmem=58,
    )


def finish(z):
    def body(s_ref, own_ref, mix_ref, mb_ref, st_ref, a_ref, out_ref):
        h = z.half
        outer = own_ref[0 : z.group, :]
        high = outer.astype(BF).astype(F32)
        ends = mm(jnp.concatenate([high, outer - high], axis=0).astype(BF), mix_ref[...], 1, 1)
        ends = ends[0 : z.group] + ends[z.group :] + own_ref[8 : 8 + z.group, 0:1] * mb_ref[...]
        base = z.tap(1)
        a = a_ref[...]
        front = jnp.zeros((z.group, z.res), F32)
        for j in range(h + 1):
            if j < h:
                column = a[:, base + j : base + j + 1] + a[:, base + h + j : base + h + j + 1]
            else:
                column = a[:, base + 3 * h : base + 3 * h + 1]
            front = front + column * st_ref[j : j + 1, :]
        out_ref[0:8, :] = ends[:, 0 : z.res] + front
        out_ref[8:16, :] = jnp.zeros((8, z.res), F32)
        out_ref[8:16, 0 : z.skip] = ends[:, z.res :]

    return call(
        body,
        "finish",
        jax.ShapeDtypeStruct((16, z.res), F32),
        [],
        in_specs=[whole()] * 5,
        out_specs=whole(),
        flops=1e7,
        nbytes=MIB,
    )


def permute(z, block, move):
    pairs = []
    for dp in range(z.data):
        for li in range(z.cycle):
            to = move(dp, li)
            if to is not None:
                pairs.append((dp * z.cycle + li, to[0] * z.cycle + to[1]))
    return lax.ppermute(block, ("dp", "layer"), pairs)


def in_hbm(arrays):
    return [pltpu.with_memory_space_constraint(array, pltpu.HBM) for array in arrays]


def tie(value, *earlier):
    return lax.optimization_barrier((value, *earlier))[0]


def near_weights(z, in_w, group_place, prepared):
    if z.cycle != 4:
        ready = prepared()
        gathered = lax.all_gather(in_w, "layer")
        return ready, layer_packs(z, ready[0]), [gathered], gathered
    rows = z.gate // 2
    part = lax.dynamic_slice_in_dim(in_w, (group_place & 1) * rows, rows, 0)
    far = permute(z, part, lambda dp, li: (dp, li ^ 2) if li in (1, 2) else None)
    near = permute(z, in_w, lambda dp, li: (dp, li ^ 1))
    ready = prepared()
    packs = layer_packs(z, ready[0])
    far = tie(far, ready[1], packs[1])
    beside = permute(z, far, lambda dp, li: (dp ^ 1, li) if li in (3, 0) else None)
    far_late = permute(z, tie(in_w, far, packs[2]), lambda dp, li: (dp, li ^ 2) if li in (3, 0) else None)
    across = lambda dp, li: (dp, li ^ 1) if li in (3, 0) else None
    cross, cross_beside = permute(z, far, across), permute(z, beside, across)
    return ready, packs, [in_w, near, far, beside, cross, cross_beside], far_late


def late_weights(z, sources, far, token):
    if z.cycle != 4:
        return sources
    far = tie(far, token)
    return [*sources[:2], far, permute(z, far, lambda dp, li: (dp, li ^ 1) if li in (1, 2) else None)]


def layer_packs(z, pack):
    if z.cycle != 4:
        return [lax.all_gather(pack, "layer")]
    near = permute(z, pack, lambda dp, li: (dp, li ^ 1))
    far = permute(z, pack, lambda dp, li: (dp, li ^ 2))
    cross = permute(z, far, lambda dp, li: (dp, li ^ 1))
    return [pack, near, far, cross]


def add(*terms):
    total = terms[0].astype(F32)
    for term in terms[1:]:
        total = total + term.astype(F32)
    return total


def sent(z, blocks, *moves):
    many = isinstance(blocks, list)
    blocks = blocks if many else [blocks]
    got = yield blocks, [permute(z, block, move) for block, move in zip(blocks, moves)]
    return got if many else got[0]


def meet_core(z, stay, cross):
    got = yield from sent(z, cross, lambda dp, li: (dp, li ^ 1))
    count = z.data // 2
    if stay.ndim == 3:
        stay, got = stay[None], got[None]
    near = [add(stay[role, :count], got[role, :count]).astype(BF) for role in range(stay.shape[0])]
    far = [add(stay[role, count:], got[role, count:]).astype(BF) for role in range(stay.shape[0])]
    return near, far


def reduce_chips(z, side, at_home, operands):
    near, far, near_other, far_other = operands
    count = z.data // 2
    away = (lambda li: not at_home(li)) if near is near_other else at_home
    by_y, by_x, by_both = yield from sent(
        z,
        [far, near_other, far_other],
        lambda dp, li: (dp, li ^ 2) if at_home(li) else None,
        lambda dp, li: (dp ^ 1, li ^ 1) if away(li) else None,
        lambda dp, li: (dp ^ 1, li ^ 3) if away(li) else None,
    )
    parts = [near, by_y, by_x, by_both]
    for b in range(1, z.bits):
        count //= 2
        send = add(*(part[count:] for part in parts)).astype(BF)
        keep = add(*(part[:count] for part in parts)).astype(BF)
        got = yield from sent(z, send, lambda dp, li: (dp ^ (1 << b), li) if at_home(li) else None)
        parts = [keep, got]
    total = add(keep[0], got[0])
    got = yield from sent(
        z, total.astype(BF), lambda dp, li: (dp, li ^ 2) if at_home(li) and (li & 2) != side else None
    )
    return total, got.astype(F32)


def reduce_last_two(z, stay, cross):
    near, far = yield from meet_core(z, stay, cross)
    operands = (near[0], far[0], near[1], far[1])
    total, got = yield from reduce_chips(z, 2, lambda li: True, operands)
    return jnp.concatenate([total, got], axis=0)


def reduce_first_two(z, stay, cross):
    near, far = yield from meet_core(z, stay, cross)
    operands = (near[0], far[0], near[0], far[0])
    total, got = yield from reduce_chips(z, 0, lambda li: (li & 1) == 1, operands)
    cut = z.share_rows // 2
    share = jnp.concatenate([total[cut:], got[cut:]], axis=0)
    share = yield from sent(z, share.astype(BF), lambda dp, li: (dp, 0) if li == 1 else None)
    return share.astype(F32), jnp.concatenate([total[:cut], got[:cut]], axis=0)


def sum_of_own_layer(z, stacked, place):
    bit = 0
    while (1 << bit) < z.cycle:
        mine = (place >> bit) & 1
        pairs = stacked.reshape((stacked.shape[0] // 2, 2) + stacked.shape[1:])
        own = lax.dynamic_index_in_dim(pairs, mine, 1, keepdims=False)
        other = lax.dynamic_index_in_dim(pairs, 1 - mine, 1, keepdims=False)
        got = yield from sent(z, other, lambda dp, li: (dp, li ^ (1 << bit)))
        stacked = own + got
        bit += 1
    return stacked[0]


class Chain:
    def __init__(self, steps):
        self.steps, self.result = steps, None
        self.leaving, self.arriving = next(steps)

    def go_on(self, arrived):
        try:
            self.leaving, self.arriving = self.steps.send(arrived)
        except StopIteration as end:
            self.leaving, self.arriving, self.result = [], [], end.value


def advance(chains, *tokens):
    chains = [chain for chain in chains if chain.arriving]
    if not chains:
        return []
    sizes = [len(chain.arriving) for chain in chains]
    arrived = list(lax.optimization_barrier((*sum((chain.arriving for chain in chains), []), *tokens)))
    marks = [arrived[0]]
    for chain, size in zip(chains, sizes):
        chain.go_on(arrived[:size])
        arrived = arrived[size:]
    return marks


def reduce_whole(z, stay, cross):
    rows = jnp.concatenate([stay, cross], axis=0)
    rows = rows.reshape(z.blocks, 2 * rows.shape[1], LANES)
    at = rows.shape[1] - z.share_first
    mix = rows[:, at + z.x_rows :].reshape(z.blocks, z.m_fold, z.m_rows, LANES)
    mix = mix.transpose(0, 2, 1, 3).reshape(z.mixed_rows, z.res)
    bias = rows[:, at + z.x_rows - 1, : z.m_rows].reshape(z.mixed_rows)
    wide = rows[:, : at + z.x_rows].transpose(0, 2, 1).reshape(z.gate, at + z.x_rows)
    out = []
    for part in (wide, mix, bias):
        part = lax.psum(part.astype(F32), "layer").astype(BF)
        out.append(lax.psum_scatter(part, "dp", scatter_dimension=0, tiled=True).astype(F32))
    return tuple(out)


def sum_of_all(z, values):
    moves = [(0, 1)]
    moves += [(1 << b, 0) for b in range(1, z.data.bit_length() - 1)] + [(1, 0)]
    moves += [(0, 1 << b) for b in range(1, z.cycle.bit_length() - 1)]
    for a, b in moves:
        values = values + (yield from sent(z, values, lambda dp, li: (dp ^ a, li ^ b)))
    return values


def per_device(*args):
    (
        audio_in,
        mel_spec,
        lengths,
        z_cotangent,
        det_cotangent,
        lu_weight,
        start_weight,
        start_bias,
        in_weight,
        cond_weight,
        gate_bias,
        mix_weight,
        mix_bias,
        end_weight,
        end_bias,
    ) = args
    cycle, data = lax.axis_size("layer"), lax.axis_size("dp")
    z = Sizes(args, cycle, data)
    place, group_place = lax.axis_index("layer"), lax.axis_index("dp")
    scalars = jnp.stack([place, group_place, place // z.copies]).astype(jnp.int32)
    in_w, mix = in_weight[0], mix_weight[0]
    start_rows = jnp.concatenate([start_weight.T, start_bias[None], jnp.zeros((7 - z.half, z.res), F32)], axis=0)
    det_row = det_cotangent[None, :]
    ends = jnp.concatenate([end_weight, end_weight, end_weight, jnp.zeros((LANES - z.group, z.mixed_rows), BF)], axis=0)

    def prepared():
        pack, start_x = prepare_weights(z, in_w, cond_weight, gate_bias, mix, mix_bias, start_rows, end_weight)(
            scalars, in_w, cond_weight[0], gate_bias, mix, mix_bias, start_rows, end_weight
        )
        x, mixed, masks, turned, matrix = prepare_frames(z)(scalars, lengths, audio_in, mel_spec, lu_weight)
        return pack, x, start_x, mixed, masks, turned, matrix

    (_, x, start_x, mixed, masks, turned, matrix), packs, early, far_late = near_weights(
        z, in_w, group_place, prepared
    )

    packs, (x, masks, turned) = in_hbm(packs), in_hbm((x, masks, turned))
    *saved, totals = forward_group(z, len(early), len(packs))(scalars, *early, *packs, x, masks, start_x)
    saved = [in_hbm(saved[4 * layer : 4 * layer + 4]) for layer in range(cycle - 1)]
    late = late_weights(z, early, far_late, totals)

    own = None
    if z.copies > 1:
        own = ((place % z.copies) == 0).astype(F32)
    mine = lambda v: v if own is None else (v * own.astype(v.dtype))
    blocks, after = {}, []
    for high in range(cycle - 1, 0, -2):
        low = high - 1
        if z.direct and not low:
            while own_outer.result is None:
                advance([own_outer])
            advance([pair], own_outer.result)
            after = [*pair.leaving]
        at_high = late if high == cycle - 1 else early
        at_low = late if low == 0 else early
        kernel = gradient_group(z, high, len(after), len(at_high), len(at_low), len(packs))
        ins = [*after, *at_high, *at_low, *packs, x, masks, ends, saved[low][3]]
        if high == cycle - 1:
            ins += [totals, z_cotangent, det_row, mixed, end_bias[:, None], lu_weight]
            ins += [saved[other][0] for other in range(cycle - 2)]
        else:
            ins += in_hbm([dres, h, dx]) + saved[high][:3]
        ins += saved[low][:3]
        if low:
            ins += [saved[low - 1][3], turned]
        else:
            ins += [turned, start_x, base, matrix, audio_in, lu_weight, det_row]
        stay, cross, *outs = kernel(scalars, *ins)
        blocks[high] = (mine(stay), mine(cross))
        if low:
            h, dx, *outs = outs
        else:
            tail, mel_grad, audio_grad = outs
        if high == cycle - 1:
            outer, a_part, latent, logdet, dres, base = outs
            dsum_rows = jnp.broadcast_to(a_part[:, z.ones : z.ones + 1], (cycle, z.group, z.res))
            own_outer = Chain(sum_of_own_layer(z, mine(jnp.concatenate([outer, dsum_rows], axis=1)), place))
            if z.direct:
                pair = Chain(reduce_last_two(z, *blocks[high]))

    if z.direct:
        token = advance([pair], tail)
        tail = tie(tail, *token)
        blocks[1] = [tie(block, *token) for block in blocks[1]]
    else:
        token = []
        while own_outer.result is None:
            token = advance([own_outer], *token)
    end_part = finish(z)(scalars, own_outer.result, mix, mix_bias, start_rows, mine(a_part))
    small = Chain(sum_of_all(z, jnp.concatenate([end_part, mine(tail)], axis=0)))
    active = [small]
    if z.direct:
        both = Chain(reduce_first_two(z, *blocks[1]))
        active += [both, pair]
        for group in ((both, small), (pair, small), (pair, small)):
            token = advance(group, *token)
    while any(chain.arriving for chain in active):
        token = advance(active, *token)
    whole_sum = small.result
    end_weight_grad = jnp.concatenate([whole_sum[0:8], whole_sum[8:16, : z.skip]], axis=1)
    lu_grad = whole_sum[24:32, : z.group]
    end_bias_grad = whole_sum[24, LANES : LANES + z.group]
    start_weight_grad = whole_sum[16 : 16 + z.half].T
    start_bias_grad = whole_sum[16 + z.half]

    if z.direct:
        first_share, share = both.result
        share = jnp.where(place >= 2, pair.result, share)
        short = jnp.where(place == 0, first_share, share[z.taps :])
        conds = short[: z.x_rows].T
        mix_grad = short[z.x_rows :].reshape(z.m_fold, z.m_rows, LANES)
        mix_grad = jnp.concatenate([mix_grad[j] for j in range(z.m_fold)], axis=1)
        mix_bias_grad = short[z.x_rows - 1, : z.m_rows]
        in_grad = share[: z.taps].T
    else:
        wide = mix_grad = mix_bias_grad = None
        for layer in range(cycle):
            high = layer + (layer + 1) % 2
            rows = z.share_rows // 2
            stay, cross = blocks[high]
            if high > 1:
                stay, cross = stay[high - layer], cross[high - layer]
            elif layer:
                stay, cross = stay[:, :rows], cross[:, :rows]
            else:
                stay, cross = stay[:, rows:], cross[:, rows:]
            new = reduce_whole(z, stay, cross)
            if not layer:
                wide, mix_grad, mix_bias_grad = (jnp.pad(new[0], ((0, 0), (z.taps, 0))), *new[1:])
                continue
            wide, mix_grad, mix_bias_grad = jax.tree.map(
                lambda now, old: jnp.where(place == layer, now, old), new, (wide, mix_grad, mix_bias_grad)
            )
        in_grad, conds = wide[:, : z.taps], wide[:, z.taps :]
    rows = conds[:, z.first : z.first + 3 * z.tap_rows].reshape(-1, 3, z.tap_rows)
    half = z.half
    rows = jnp.concatenate([rows[:, :, :half] + rows[:, :, half : 2 * half], rows[:, :, 3 * half : 3 * half + 1]], 2)
    first_in_grad = jnp.einsum("rkj,jc->rkc", rows, start_rows[: half + 1], precision=highest).reshape(-1, z.taps)
    in_grad = jnp.where(place == 0, first_in_grad, in_grad)

    def own_columns(rows):
        if z.copies == 1:
            return rows
        width = z.frames // z.copies
        return lax.dynamic_slice_in_dim(rows, (place % z.copies) * width, width, 1)

    return (
        own_columns(latent),
        own_columns(logdet)[0],
        own_columns(audio_grad),
        own_columns(mel_grad),
        lu_grad,
        start_weight_grad,
        start_bias_grad,
        in_grad[None],
        conds[None, :, : z.mel],
        conds[None, :, z.ones],
        mix_grad[None],
        mix_bias_grad[None],
        end_weight_grad,
        end_bias_grad,
    )


def solution(mesh):
    in_specs = (
        P(None, "dp"),
        P(None, "dp"),
        P("dp", None),
        P(None, "dp"),
        P("dp"),
        P(),
        P(),
        P(),
        P("layer", None, None),
        P("layer", None, None),
        P("layer", None),
        P("layer", None, None),
        P("layer", None),
        P(),
        P(),
    )
    out_specs = (
        P(None, ("dp", "layer")),
        P(("dp", "layer")),
        P(None, ("dp", "layer")),
        P(None, ("dp", "layer")),
        P(),
        P(),
        P(),
        P("layer", "dp", None),
        P("layer", "dp", None),
        P("layer", "dp"),
        P("layer", "dp", None),
        P("layer", "dp"),
        P(),
        P(),
    )
    return jax.shard_map(
        per_device, mesh=mesh, in_specs=in_specs, out_specs=out_specs, check_vma=False
    )
```
